256 devices in a mesh: dp: 8 (over x, core), proto: 32 (over y, z).
Axes of the slice: x: 4, y: 4, z: 8, core: 2. Of those that a mesh axis runs over, the one named last changes fastest.
Arguments:
- student_patches: bfloat16 [8192, 256], P('dp'), may hold values from -160 to 160
- teacher_patches: bfloat16 [8192, 256], P('dp'), may hold values from -160 to 160
- masked_index: int32 [32, 128], P('dp'), may hold values from 0 to 255, as said below
- prototypes: bfloat16 [256, 131072], P(None, 'proto'), may hold values from -2.5 to 2.5
Outputs:
- grad_patches: float32 [8192, 256], P('dp')
- grad_prototypes: float32 [256, 131072], P('dp', 'proto')
The draws below stay inside these ranges and needn't reach their ends.
Inputs may be any that keep to these rules, and one draw needn't show every extreme that they name: `masked_index`: each row holds 128 distinct patch positions of its image.
All inputs are finite; a program needn't handle non-finite values.
Results may differ from the reference program's by a relative error of at most 0.0024.
Values sent between devices are 32-bit elements; how exact they have to be, the bound alone decides.
A program may use at most 64 MiB of HBM per device.

```python
import jax
import jax.numpy as jnp
from jax import lax

D = 256
PROTOS = 131072
PATCHES = 256
MASKED = 128
ITERS = 3
IMAGES = 32
ROWS = 4096
N_PROTO = 32


def shared_direction(key):
    values = jax.random.normal(jax.random.fold_in(key, 977), (D,), jnp.float32)
    return jnp.clip(values, -3.0, 3.0)


def patch_values(key, direction, lowest, highest):
    noise_key, scale_key = jax.random.split(key)
    count = IMAGES * PATCHES
    image = (jnp.arange(count) // PATCHES).astype(jnp.float32)
    strength = lowest + (highest - lowest) * image / max(IMAGES - 1, 1)
    noise = jnp.clip(jax.random.normal(noise_key, (count, D), jnp.float32), -4.0, 4.0)
    scales = jnp.exp(jax.random.uniform(scale_key, (count,), jnp.float32, 0.0, jnp.log(10.0)))
    values = (strength[:, None] * direction[None, :] + noise) * scales[:, None]
    return values.astype(jnp.bfloat16)


def draw_student_patches(key, part):
    direction = shared_direction(key)
    key = jax.random.fold_in(key, 1)
    return patch_values(key, direction, 0.3, 1.3)


def draw_teacher_patches(key, part):
    direction = shared_direction(key)
    key = jax.random.fold_in(key, 2)
    return patch_values(key, direction, 0.5, 2.0)


def draw_prototypes(key, part):
    direction = shared_direction(key)
    key = jax.random.fold_in(key, 3)
    noise_key, scale_key = jax.random.split(key)
    tilt = 1.5 * jnp.arange(PROTOS).astype(jnp.float32) / (PROTOS - 1)
    noise = jnp.clip(jax.random.normal(noise_key, (D, PROTOS), jnp.float32), -4.0, 4.0)
    scales = jnp.exp(jax.random.uniform(scale_key, (PROTOS,), jnp.float32, jnp.log(0.5), jnp.log(4.0)))
    values = (direction[:, None] * tilt[None, :] + noise) / jnp.sqrt(D * 1.0) * scales[None, :]
    return jnp.clip(values, -2.5, 2.5).astype(jnp.bfloat16)


def draw_masked_index(key, part):
    key = jax.random.fold_in(key, 7)
    keys = jax.random.split(key, IMAGES)
    orders = jax.vmap(lambda single: jax.random.permutation(single, PATCHES))(keys).astype(jnp.int32)
    chosen = orders[:, :MASKED]
    moved = PATCHES - 1 - chosen[:, :1]
    return ((chosen + moved) % PATCHES).astype(jnp.int32)


def setup_inputs(seed: int = 0) -> dict:
    key_list = jax.random.split(jax.random.key(seed), 5)
    student_patches = draw_student_patches(jax.random.fold_in(key_list[4], 71), 0)
    teacher_patches = draw_teacher_patches(jax.random.fold_in(key_list[4], 71), 0)
    masked_index = draw_masked_index(jax.random.fold_in(key_list[4], 71), 0)
    prototypes = draw_prototypes(jax.random.fold_in(key_list[4], 71), 0)
    return {"student_patches": student_patches, "teacher_patches": teacher_patches, "masked_index": masked_index, "prototypes": prototypes}


teacher_temp = 0.07
student_temp = 0.1
loss_factor = 4096.0
epsilon = 1e-06

def unit_rows(values):
    norms = jnp.sqrt(lax.optimization_barrier(jnp.sum(values * values, axis=-1, keepdims=True)) + epsilon)
    return (values / norms, norms)

def masked_rows(patches_in, masked_index):
    images = masked_index.shape[0]
    patch_count = patches_in.shape[0] // images
    offsets = patch_count * jnp.arange(images, dtype=jnp.int32)
    positions = (masked_index + offsets[:, None]).reshape(-1).astype(jnp.int32)
    return (positions, jnp.take(patches_in, positions, axis=0).astype(jnp.float32))

def reference(student_patches, teacher_patches, masked_index, prototypes):
    positions, student = masked_rows(student_patches, masked_index)
    teacher = masked_rows(teacher_patches, masked_index)[1]
    student_unit, student_norm = unit_rows(student)
    student_cast = student_unit.astype(jnp.bfloat16)
    teacher_cast = unit_rows(teacher)[0].astype(jnp.bfloat16)
    weights = prototypes.astype(jnp.float32)
    proto_norm = jnp.sqrt(lax.optimization_barrier(jnp.sum(weights * weights, axis=0)) + epsilon)
    proto_unit = weights / proto_norm[None, :]
    proto_cast = proto_unit.astype(jnp.bfloat16)
    block_width = PROTOS // N_PROTO

    def split_cols(matrix):
        return matrix.reshape(matrix.shape[0], N_PROTO, block_width).transpose(1, 0, 2)
    cast_blocks = split_cols(proto_cast)

    def teacher_block(weight_block):
        return jnp.exp(jnp.dot(teacher_cast, weight_block, preferred_element_type=jnp.float32) / teacher_temp)
    row_scale = jnp.ones((ROWS,), jnp.float32)
    column_scale = jnp.ones((N_PROTO, block_width), jnp.float32)
    for sweep in range(ITERS):
        current = row_scale

        def balance(running, weight_block):
            expos = teacher_block(weight_block)
            column_part = 1.0 / jnp.dot(current, expos, precision=lax.Precision.HIGHEST)
            return (running + jnp.dot(expos, column_part, precision=lax.Precision.HIGHEST), column_part)
        row_sums, column_scale = lax.scan(balance, jnp.zeros((ROWS,), jnp.float32), cast_blocks)
        row_scale = 1.0 / row_sums

    def student_exp(weight_block):
        return jnp.exp(jnp.dot(student_cast, weight_block, preferred_element_type=jnp.float32) / student_temp)

    def add_totals(running, weight_block):
        return (running + lax.optimization_barrier(jnp.sum(student_exp(weight_block), axis=1)), None)
    totals = lax.scan(add_totals, jnp.zeros((ROWS,), jnp.float32), cast_blocks)[0]

    def finish(grad_unit, pieces):
        weight_block, column_part, unit_block, norm_block = pieces
        target = teacher_block(weight_block) * row_scale[:, None] * column_part[None, :]
        probs = student_exp(weight_block) / totals[:, None]
        slopes = loss_factor / student_temp * (probs - target)
        grad_unit = grad_unit + lax.dot_general(slopes, unit_block, (((1,), (1,)), ((), ())), precision=lax.Precision.HIGHEST, preferred_element_type=jnp.float32)
        weight_total = lax.dot_general(student_unit, slopes, (((0,), (0,)), ((), ())), precision=lax.Precision.HIGHEST, preferred_element_type=jnp.float32)
        inner_dot = lax.optimization_barrier(jnp.sum(unit_block * weight_total, axis=0))
        return (grad_unit, (weight_total - unit_block * inner_dot[None, :]) / norm_block[None, :])
    pieces = (cast_blocks, column_scale, split_cols(proto_unit), proto_norm.reshape(N_PROTO, block_width))
    grad_unit, grad_blocks = lax.scan(finish, jnp.zeros((ROWS, D), jnp.float32), pieces)
    grad_prototypes = grad_blocks.transpose(1, 0, 2).reshape(D, PROTOS)
    grad_rows = (grad_unit - student_unit * lax.optimization_barrier(jnp.sum(student_unit * grad_unit, axis=-1, keepdims=True))) / student_norm
    grad_patches = jnp.zeros((student_patches.shape[0], D), jnp.float32).at[positions].set(grad_rows)
    return (grad_patches, grad_prototypes)
```

```python
import math

import jax
import jax.numpy as jnp
from jax import lax
from jax.experimental import pallas as pl
from jax.experimental.pallas import tpu as pltpu
from jax.sharding import PartitionSpec as P

MESH = pl.DeviceIdType.MESH
F32 = jnp.float32
BF16 = jnp.bfloat16

teacher_scale = math.log2(math.e) / 0.07
student_scale = math.log2(math.e) / 0.1
slope_scale = 4096.0 / 0.1
epsilon = 1e-06

W = 512
NY, NZ = 4, 8
FAR_FIRST = sorted(
    [(dy, dz) for dy in range(NY) for dz in range(NZ) if dy or dz],
    key=lambda o: -(min(o[0], NY - o[0]) + min(o[1], NZ - o[1])),
)


def dot(a, b):
    return jnp.dot(a, b, preferred_element_type=F32)


def dot_cols(a, b):
    return lax.dot_general(a, b, (((1,), (1,)), ((), ())), preferred_element_type=F32)


def split(value):
    high = value.astype(BF16)
    return high, (value - high.astype(F32)).astype(BF16)


def kernel(
    student_hbm, teacher_hbm, index_hbm, protos_hbm,
    gp_ref, gw_ref,
    student_v, teacher_v, index_v, protos_v, in_sem,
    onehot, t_send, s_send, t_other, s_other, t_cast, s_cast, s_unit_t, s_inv,
    pc, plo, pinv, expos,
    e2h, e2l, x2h, x2l, wtp, a_hi, a_lo,
    cbuf, c_ssem, c_rsem,
    r1buf, r2buf, r3buf, r_ssem, r_rsem, ub, vrow, tot_row, tot_acc, totb,
    ts_ssem, ts_rsem, swap_s, swap_r, swap_ssem, swap_rsem,
    fp, ft, yr, ysum, y_ssem, y_rsem, zr, z_ssem, z_rsem,
    ag, agz_ssem, agz_rsem, agy_ssem, agy_rsem,
    gpart, p1r, p1_ssem, p1_rsem, p2r, p2_ssem, p2_rsem,
    fin_s, fin_r, fin_ssem, fin_rsem,
):
    dp = lax.axis_index("dp")
    pr = lax.axis_index("proto")
    x, core = lax.div(dp, 2), lax.rem(dp, 2)
    y, z = lax.div(pr, NZ), lax.rem(pr, NZ)
    x_next, x_prev, x_far = lax.rem(x + 1, 4), lax.rem(x + 3, 4), lax.rem(x + 2, 4)
    right = (x_next * 2 + core, pr)
    left = (x_prev * 2 + core, pr)
    partner = (x * 2 + 1 - core, pr)

    def dp_peer(k):
        return (lax.rem(dp + k, 8), pr)

    def proto_peer(dy, dz):
        return (dp, lax.rem(y + dy, NY) * NZ + lax.rem(z + dz, NZ))

    def remote(src, dst, ssem, rsem, device):
        return pltpu.make_async_remote_copy(
            src, dst, ssem, rsem, device_id=device, device_id_type=MESH
        )

    def wait_bytes(ref, sem):
        pltpu.make_async_copy(ref, ref, sem).wait()

    barrier = pltpu.get_barrier_semaphore()
    for k in range(1, 8):
        pl.semaphore_signal(barrier, inc=1, device_id=dp_peer(k), device_id_type=MESH)
    for dy, dz in FAR_FIRST:
        pl.semaphore_signal(
            barrier, inc=1, device_id=proto_peer(dy, dz), device_id_type=MESH
        )
    loads = [
        pltpu.make_async_copy(src, dst, in_sem.at[i])
        for i, (src, dst) in enumerate(
            [(index_hbm, index_v), (teacher_hbm, teacher_v), (protos_hbm, protos_v), (student_hbm, student_v)]
        )
    ]
    for load in loads:
        load.start()

    loads[0].wait()
    for i in range(4):
        places = lax.broadcasted_iota(jnp.int32, (256, 128), 0)
        onehot[i] = jnp.where(places == index_v[i : i + 1, :], 1.0, 0.0).astype(BF16)

    def masked(patches, i):
        rows = lax.dot_general(
            onehot[i], patches[256 * i : 256 * i + 256, :],
            (((0,), (0,)), ((), ())), preferred_element_type=F32,
        )
        norm = jnp.sqrt(jnp.sum(rows * rows, axis=1, keepdims=True) + epsilon)
        return rows / norm, norm

    loads[1].wait()
    for i in range(4):
        unit, _ = masked(teacher_v, i)
        t_send[128 * i : 128 * i + 128, :] = unit
        t_cast[128 * i : 128 * i + 128, :] = unit.astype(BF16)

    def put_cols(buf, slot, j, sums):
        for q in range(W // 128):
            buf[slot, pl.ds(4 * j + q, 1), :] = sums[:, 128 * q : 128 * q + 128]

    loads[2].wait()

    def front(j, carry):
        cols = pl.ds(pl.multiple_of(j * W, W), W)
        weights = protos_v[:, cols].astype(F32)
        inv = 1.0 / jnp.sqrt(jnp.sum(weights * weights, axis=0, keepdims=True) + epsilon)
        pinv[:, cols] = inv
        high, low = split(weights * inv)
        pc[:, cols] = high
        plo[:, cols] = low
        block = jnp.exp2(dot(t_cast[...], high) * teacher_scale)
        expos[:, cols] = block
        put_cols(cbuf.at[0], dp, j, jnp.sum(block, axis=0, keepdims=True))
        return carry

    lax.fori_loop(0, 8, front, 0)
    pl.semaphore_wait(barrier, 7 + len(FAR_FIRST))

    def send_cols(t):
        for k in (4, 3, 5, 2, 6, 1, 7):
            remote(cbuf.at[t, dp], cbuf.at[t, dp], c_ssem.at[t], c_rsem.at[t], dp_peer(k)).start()

    def take_cols(t):
        wait_bytes(cbuf.at[t, pl.ds(0, 7)], c_rsem.at[t])
        vrow[...] = 1.0 / jnp.sum(cbuf[t], axis=0)

    def send_rows(buf, t):
        for dy, dz in FAR_FIRST:
            remote(buf.at[pr], buf.at[pr], r_ssem.at[t], r_rsem.at[t], proto_peer(dy, dz)).start()

    def take_rows(buf, t):
        wait_bytes(buf.at[pl.ds(0, 31)], r_rsem.at[t])
        return jnp.sum(buf[...], axis=0)

    def spread(row):
        return jnp.transpose(jnp.broadcast_to(row, (128, 128)))

    def row_pass(buf):
        def image(i, carry):
            rows = pl.ds(pl.multiple_of(i * 128, 128), 128)
            total = expos[rows, 0:128] * vrow[0:1, :]
            for k in range(1, 32):
                total += expos[rows, 128 * k : 128 * k + 128] * vrow[k : k + 1, :]
            buf[pr, pl.ds(i, 1), :] = jnp.sum(jnp.transpose(total), axis=0, keepdims=True)
            return carry

        lax.fori_loop(0, 4, image, 0)

    def col_pass(t):
        def chunk(k, carry):
            cols = pl.ds(pl.multiple_of(k * 128, 128), 128)
            cbuf[t, dp, pl.ds(k, 1), :] = jnp.sum(
                expos[:, cols] * ub[...], axis=0, keepdims=True
            )
            return carry

        lax.fori_loop(0, 32, chunk, 0)

    def spread_rows(values, target):
        for i in range(4):
            target[128 * i : 128 * i + 128, :] = spread(values[i : i + 1, :])

    send_cols(0)
    loads[3].wait()
    for i in range(4):
        unit, norm = masked(student_v, i)
        rows = slice(128 * i, 128 * i + 128)
        s_send[rows, :] = unit
        s_cast[rows, :] = unit.astype(BF16)
        s_inv[rows, :] = jnp.broadcast_to(1.0 / norm, (128, 128))
        s_unit_t[:, rows] = jnp.transpose(unit)
    ts = [
        remote(t_send, t_other, ts_ssem.at[0], ts_rsem.at[0], partner),
        remote(s_send, s_other, ts_ssem.at[1], ts_rsem.at[1], partner),
    ]
    take_cols(0)
    row_pass(r1buf)
    send_rows(r1buf, 0)
    for copy in ts:
        copy.start()

    half = core * 2048
    tot_acc[...] = jnp.zeros_like(tot_acc)
    fp[...] = jnp.zeros_like(fp)

    def student_cols(j, keep):
        at = lax.rem(j * W + half, 4096)
        cols = pl.ds(pl.multiple_of(at, W), W)
        block = jnp.exp2(dot(s_cast[...], pc[:, cols]) * student_scale)
        for q in range(W // 128):
            tot_acc[...] += block[:, 128 * q : 128 * q + 128]
        high, low = split(block)
        if keep:
            mine = pl.ds(pl.multiple_of(j * W, W), W)
            x2h[0:512, mine] = high
            x2l[0:512, mine] = low
        fp[...] += (
            dot_cols(high, pc[:, cols]) + dot_cols(low, pc[:, cols]) + dot_cols(high, plo[:, cols])
        )

    def student_mine(j, carry):
        student_cols(j, True)
        return carry

    def student_rest(j, carry):
        student_cols(j, False)
        return carry

    lax.fori_loop(0, 4, student_mine, 0)
    lax.fori_loop(4, 8, student_rest, 0)
    for i in range(4):
        r2buf[pr, 4 + i : 5 + i, :] = jnp.sum(
            jnp.transpose(tot_acc[128 * i : 128 * i + 128, :]), axis=0, keepdims=True
        )
    spread_rows(1.0 / take_rows(r1buf, 0), ub)
    col_pass(1)

    send_cols(1)
    for copy in ts:
        copy.wait_recv()
    t_cast[...] = t_other[...].astype(BF16)
    s_cast[...] = s_other[...].astype(BF16)

    def own_split(j, carry):
        cols = pl.ds(pl.multiple_of(j * W + half, W), W)
        mine = pl.ds(pl.multiple_of(j * W, W), W)
        high, low = split(expos[:, cols])
        e2h[0:512, mine] = high
        e2l[0:512, mine] = low
        return carry

    lax.fori_loop(0, 4, own_split, 0)
    for i in range(4):
        s_unit_t[:, 512 + 128 * i : 640 + 128 * i] = jnp.transpose(
            s_other[128 * i : 128 * i + 128, :]
        )
    take_cols(1)
    row_pass(r2buf)
    send_rows(r2buf, 1)

    def send_y(q, src):
        for dy in (2, 1, 3):
            ty = lax.rem(y + dy, NY)
            remote(
                src.at[pl.ds(pl.multiple_of(ty * 128, 128), 128)], yr.at[q, dy - 1],
                y_ssem.at[q], y_rsem.at[q], proto_peer(dy, 0),
            ).start()

    def take_y(q, src):
        wait_bytes(yr.at[q], y_rsem.at[q])
        own = pl.ds(pl.multiple_of(y * 128, 128), 128)
        ysum[q] = src[own, :] + yr[q, 0] + yr[q, 1] + yr[q, 2]

    def send_z(q):
        for dz in (4, 3, 5, 2, 6, 1, 7):
            tz = lax.rem(z + dz, NZ)
            remote(
                ysum.at[q, pl.ds(pl.multiple_of(tz * 16, 16), 16)], zr.at[q, dz - 1],
                z_ssem.at[q], z_rsem.at[q], proto_peer(0, dz),
            ).start()

    def take_z(q):
        wait_bytes(zr.at[q], z_rsem.at[q])
        total = ysum[q, pl.ds(pl.multiple_of(z * 16, 16), 16), :]
        for k in range(7):
            total += zr[q, k]
        return total

    def other_cols(j, carry):
        cols = pl.ds(pl.multiple_of(j * W + half, W), W)
        mine = pl.ds(pl.multiple_of(j * W, W), W)
        high, low = split(jnp.exp2(dot(t_cast[...], pc[:, cols]) * teacher_scale))
        e2h[512:1024, mine] = high
        e2l[512:1024, mine] = low
        high, low = split(jnp.exp2(dot(s_cast[...], pc[:, cols]) * student_scale))
        x2h[512:1024, mine] = high
        x2l[512:1024, mine] = low
        return carry

    lax.fori_loop(0, 4, other_cols, 0)
    sums = take_rows(r2buf, 1)
    spread_rows(1.0 / sums[0:4, :], ub)
    tot_row[...] = 1.0 / sums[4:8, :]
    col_pass(2)

    send_cols(2)
    swap_s[0] = tot_row[...]
    swap_tot = remote(swap_s.at[0], swap_r.at[0], swap_ssem.at[0], swap_rsem.at[0], partner)
    swap_tot.start()
    send_y(0, fp)
    spread_rows(tot_row[...], totb)
    swap_tot.wait_recv()

    def scale_rows(own_ref, other_ref):
        for i in range(4):
            cols = slice(128 * i, 128 * i + 128)
            high, low = split(s_unit_t[:, cols] * own_ref[i : i + 1, :])
            a_hi[:, cols] = high
            a_lo[:, cols] = low
            cols = slice(512 + 128 * i, 640 + 128 * i)
            high, low = split(s_unit_t[:, cols] * other_ref[i : i + 1, :])
            a_hi[:, cols] = high
            a_lo[:, cols] = low

    def weigh(high, low, cols):
        return (
            dot(a_hi[...], high[:, cols]) + dot(a_lo[...], high[:, cols]) + dot(a_hi[...], low[:, cols])
        )

    scale_rows(tot_row, swap_r.at[0])

    def probs_part(j, carry):
        mine = pl.ds(pl.multiple_of(j * W, W), W)
        wtp[:, mine] = weigh(x2h, x2l, mine)
        return carry

    lax.fori_loop(0, 4, probs_part, 0)
    take_cols(2)
    row_pass(r3buf)
    send_rows(r3buf, 2)

    ft[...] = jnp.zeros_like(ft)

    def target_cols(j, carry):
        cols = pl.ds(pl.multiple_of(j * W, W), W)
        unit = pc[:, cols].astype(F32) + plo[:, cols].astype(F32)
        scaled = jnp.concatenate(
            [
                unit[:, 128 * q : 128 * q + 128] * vrow[pl.ds(4 * j + q, 1), :]
                for q in range(W // 128)
            ],
            axis=1,
        )
        b_high, b_low = split(scaled)
        high, low = split(expos[:, cols])
        ft[...] += dot_cols(high, b_high) + dot_cols(low, b_high) + dot_cols(high, b_low)
        return carry

    lax.fori_loop(0, 8, target_cols, 0)
    take_y(0, fp)
    send_z(0)
    send_y(1, ft)
    swap_s[1] = 1.0 / take_rows(r3buf, 2)
    swap_u = remote(swap_s.at[1], swap_r.at[1], swap_ssem.at[1], swap_rsem.at[1], partner)
    swap_u.start()
    spread_rows(swap_s[1], ub)
    swap_u.wait_recv()
    scale_rows(swap_s.at[1], swap_r.at[1])

    def block(d, offset, size):
        return pl.ds(pl.multiple_of(d * 64 + offset, 32), size)

    def protos_part(j, carry):
        mine = pl.ds(pl.multiple_of(j * W, W), W)
        cols = pl.ds(pl.multiple_of(j * W + half, W), W)
        target = weigh(e2h, e2l, mine)
        at = half // 128 + 4 * j
        target = jnp.concatenate(
            [
                target[:, 128 * q : 128 * q + 128] * vrow[pl.ds(at + q, 1), :]
                for q in range(W // 128)
            ],
            axis=1,
        )
        total = wtp[:, mine] - target
        unit = pc[:, cols].astype(F32) + plo[:, cols].astype(F32)
        inner = jnp.sum(unit * total, axis=0, keepdims=True)
        gpart[j] = (total - unit * inner) * (pinv[:, cols] * slope_scale)
        remote(gpart.at[j, block(x_far, 0, 32)], p1r.at[j, 0], p1_ssem.at[j, 0], p1_rsem.at[j, 0], right).start()
        remote(gpart.at[j, block(x_far, 32, 32)], p1r.at[j, 1], p1_ssem.at[j, 1], p1_rsem.at[j, 1], left).start()
        return carry

    lax.fori_loop(0, 4, protos_part, 0)

    def pass_on(j, carry):
        wait_bytes(p1r.at[j, 0], p1_rsem.at[j, 0])
        gpart[j, block(x_next, 0, 32), :] += p1r[j, 0]
        remote(gpart.at[j, block(x_next, 0, 64)], p2r.at[j, 0], p2_ssem.at[j, 0], p2_rsem.at[j, 0], right).start()
        wait_bytes(p1r.at[j, 1], p1_rsem.at[j, 1])
        gpart[j, block(x_prev, 32, 32), :] += p1r[j, 1]
        remote(gpart.at[j, block(x_prev, 0, 64)], p2r.at[j, 1], p2_ssem.at[j, 1], p2_rsem.at[j, 1], left).start()
        return carry

    lax.fori_loop(0, 4, pass_on, 0)

    take_y(1, ft)
    send_z(1)
    own16 = pl.ds(pl.multiple_of(y * 128 + z * 16, 16), 16)
    by_probs = take_z(0)
    by_target = take_z(1)
    unit = s_send[own16, :]
    scale_p = jnp.concatenate([totb[own16, :]] * 2, axis=1)
    scale_t = jnp.concatenate([ub[own16, :]] * 2, axis=1)
    grad = slope_scale * (by_probs * scale_p - by_target * scale_t)
    inner = jnp.sum(unit * grad, axis=1, keepdims=True)
    ag[y, z] = (grad - unit * inner) * jnp.concatenate([s_inv[own16, :]] * 2, axis=1)
    for dz in (4, 3, 5, 2, 6, 1, 7):
        remote(ag.at[y, z], ag.at[y, z], agz_ssem, agz_rsem, proto_peer(0, dz)).start()

    def finish(j, carry):
        wait_bytes(p2r.at[j, 0], p2_rsem.at[j, 0])
        wait_bytes(p2r.at[j, 1], p2_rsem.at[j, 1])

        def rows_of(c):
            at = pl.multiple_of(c * 32, 32)
            return (
                gpart[j, block(x, at, 32), :] + p2r[j, 0, pl.ds(at, 32), :] + p2r[j, 1, pl.ds(at, 32), :]
            )

        fin_s[j] = rows_of(1 - core)
        remote(fin_s.at[j], fin_r.at[j], fin_ssem.at[j], fin_rsem.at[j], partner).start()
        gw_ref[:, pl.ds(pl.multiple_of(j * W + half, W), W)] = rows_of(core)
        return carry

    lax.fori_loop(0, 2, finish, 0)
    wait_bytes(ag.at[y, pl.ds(0, 7)], agz_rsem)
    for dy in (2, 1, 3):
        remote(ag.at[y], ag.at[y], agy_ssem, agy_rsem, proto_peer(dy, 0)).start()
    lax.fori_loop(2, 4, finish, 0)

    def finish_other(j, carry):
        wait_bytes(fin_r.at[j], fin_rsem.at[j])
        at = pl.multiple_of(j * W + 2048 - half, W)
        gw_ref[:, pl.ds(at, W)] = fin_r[j]
        return carry

    lax.fori_loop(0, 4, finish_other, 0)
    wait_bytes(ag.at[pl.ds(0, 3)], agy_rsem)
    for i in range(4):
        rows = ag[i].reshape(128, 256)
        high, low = split(rows)
        rest = (rows - high.astype(F32) - low.astype(F32)).astype(BF16)
        gp_ref[256 * i : 256 * i + 256, :] = (
            dot(onehot[i], high) + dot(onehot[i], low) + dot(onehot[i], rest)
        )

    for t in range(3):
        wait_bytes(cbuf.at[t, pl.ds(0, 7)], c_ssem.at[t])
        buf = (r1buf, r2buf, r3buf)[t]
        wait_bytes(buf.at[pl.ds(0, 31)], r_ssem.at[t])
    for copy in ts:
        copy.wait_send()
    swap_tot.wait_send()
    swap_u.wait_send()
    for q in range(2):
        wait_bytes(yr.at[q], y_ssem.at[q])
        wait_bytes(zr.at[q], z_ssem.at[q])
    wait_bytes(ag.at[0, pl.ds(0, 7)], agz_ssem)
    wait_bytes(ag.at[pl.ds(0, 3)], agy_ssem)

    def drain(j, carry):
        for s in range(2):
            wait_bytes(p1r.at[j, s], p1_ssem.at[j, s])
            wait_bytes(p2r.at[j, s], p2_ssem.at[j, s])
        wait_bytes(fin_s.at[j], fin_ssem.at[j])
        return carry

    lax.fori_loop(0, 4, drain, 0)


def body(student_patches, teacher_patches, masked_index, prototypes):
    dma = pltpu.SemaphoreType.DMA

    def vmem(*shape, dtype=F32):
        return pltpu.VMEM(shape, dtype)

    def half_vmem(*shape):
        return pltpu.VMEM(shape, BF16)

    scratch = [
        half_vmem(1024, 256), half_vmem(1024, 256), vmem(4, 128, dtype=jnp.int32), half_vmem(256, 4096), dma((4,)),
        half_vmem(4, 256, 128), vmem(512, 256), vmem(512, 256), vmem(512, 256), vmem(512, 256),
        half_vmem(512, 256), half_vmem(512, 256), vmem(256, 1024), vmem(512, 128),
        half_vmem(256, 4096), half_vmem(256, 4096), vmem(1, 4096), vmem(512, 4096),
        half_vmem(1024, 2048), half_vmem(1024, 2048), half_vmem(1024, 2048), half_vmem(1024, 2048),
        vmem(256, 2048), half_vmem(256, 1024), half_vmem(256, 1024),
        vmem(3, 8, 32, 128), dma((3,)), dma((3,)),
        vmem(32, 4, 128), vmem(32, 8, 128), vmem(32, 4, 128), dma((3,)), dma((3,)),
        vmem(512, 128), vmem(32, 128), vmem(4, 128), vmem(512, 128), vmem(512, 128),
        dma((2,)), dma((2,)), vmem(2, 4, 128), vmem(2, 4, 128), dma((2,)), dma((2,)),
        vmem(512, 256), vmem(512, 256), vmem(2, 3, 128, 256), vmem(2, 128, 256), dma((2,)), dma((2,)),
        vmem(2, 7, 16, 256), dma((2,)), dma((2,)),
        vmem(4, 8, 16, 256), dma, dma, dma, dma,
        vmem(4, 256, 512), vmem(4, 2, 32, 512), dma((4, 2)), dma((4, 2)),
        vmem(4, 2, 64, 512), dma((4, 2)), dma((4, 2)),
        vmem(4, 32, 512), vmem(4, 32, 512), dma((4,)), dma((4,)),
    ]
    return pl.pallas_call(
        kernel,
        out_shape=(
            jax.ShapeDtypeStruct((1024, 256), F32),
            jax.ShapeDtypeStruct((32, 4096), F32),
        ),
        in_specs=[pl.BlockSpec(memory_space=pl.ANY)] * 4,
        out_specs=(pl.BlockSpec(memory_space=pltpu.VMEM), pl.BlockSpec(memory_space=pltpu.VMEM)),
        scratch_shapes=scratch,
        compiler_params=pltpu.CompilerParams(
            collective_id=0, has_side_effects=True, vmem_limit_bytes=60 * 1024 * 1024
        ),
    )(student_patches, teacher_patches, masked_index, prototypes)


def solution(mesh):
    placed = (P("dp", None), P("dp", None), P("dp", None), P(None, "proto"))
    return jax.shard_map(
        body,
        mesh=mesh,
        in_specs=placed,
        out_specs=(P("dp", None), P("dp", "proto")),
        check_vma=False,
    )
```

```python
import math

import jax
import jax.numpy as jnp
from jax import lax
from jax.experimental import pallas as pl
from jax.experimental.pallas import tpu as pltpu
from jax.sharding import PartitionSpec as P

MESH = pl.DeviceIdType.MESH
F32 = jnp.float32
BF16 = jnp.bfloat16

teacher_scale = math.log2(math.e) / 0.07
student_scale = math.log2(math.e) / 0.1
slope_scale = 4096.0 / 0.1
epsilon = 1e-06

W = 512
V = 256
NY, NZ = 4, 8
FAR_FIRST = sorted(
    [(dy, dz) for dy in range(NY) for dz in range(NZ) if dy or dz],
    key=lambda o: -(min(o[0], NY - o[0]) + min(o[1], NZ - o[1])),
)


def dot(a, b):
    return jnp.dot(a, b, preferred_element_type=F32)


def dot_cols(a, b):
    return lax.dot_general(a, b, (((1,), (1,)), ((), ())), preferred_element_type=F32)


def split(value):
    high = value.astype(BF16)
    return high, (value - high.astype(F32)).astype(BF16)


def kernel(
    student_hbm, teacher_hbm, index_hbm, protos_hbm,
    rows_hbm, gw_hbm,
    student_v, teacher_v, index_v, protos_v, in_sem,
    onehot, t_send, s_send, t_other, s_other, t_cast, s_cast, s_unit_t, s_inv,
    pc, plo, pinv, expos,
    e2h, e2l, x2h, x2l, wtp, a_hi, a_lo,
    cbuf, c_ssem, c_rsem,
    r1buf, r2buf, r3buf, tbuf, r_ssem, r_rsem, ub, vrow, tot_row, tot_acc, totb,
    ts_ssem, ts_rsem, swap_s, swap_r, swap_ssem, swap_rsem,
    fp, ft, yr, ysum, y_ssem, y_rsem, zr, z_ssem, z_rsem,
    ag, agz_ssem, agz_rsem, agy_ssem, agy_rsem,
    gpart, p1r, p1_ssem, p1_rsem, p2r, p2_ssem, p2_rsem,
    fin_s, fin_r, fin_ssem, fin_rsem, gw_ref, out_sem,
):
    dp = lax.axis_index("dp")
    pr = lax.axis_index("proto")
    x, core = lax.div(dp, 2), lax.rem(dp, 2)
    y, z = lax.div(pr, NZ), lax.rem(pr, NZ)
    x_next, x_prev, x_far = lax.rem(x + 1, 4), lax.rem(x + 3, 4), lax.rem(x + 2, 4)
    right = (x_next * 2 + core, pr)
    left = (x_prev * 2 + core, pr)
    partner = (x * 2 + 1 - core, pr)

    def dp_peer(k):
        return (lax.rem(dp + k, 8), pr)

    def proto_peer(dy, dz):
        return (dp, lax.rem(y + dy, NY) * NZ + lax.rem(z + dz, NZ))

    def remote(src, dst, ssem, rsem, device):
        return pltpu.make_async_remote_copy(
            src, dst, ssem, rsem, device_id=device, device_id_type=MESH
        )

    def wait_bytes(ref, sem):
        pltpu.make_async_copy(ref, ref, sem).wait()

    def load(src, dst, sem, parts):
        size = src.shape[0] // parts
        for i in range(parts):
            rows = pl.ds(i * size, size)
            pltpu.make_async_copy(src.at[rows], dst.at[rows], sem).start()

    load(index_hbm, index_v, in_sem.at[0], 1)
    load(teacher_hbm, teacher_v, in_sem.at[1], 4)
    load(protos_hbm, protos_v, in_sem.at[2], 8)
    load(student_hbm, student_v, in_sem.at[3], 4)
    barrier = pltpu.get_barrier_semaphore()
    for k in range(1, 8):
        pl.semaphore_signal(barrier, inc=1, device_id=dp_peer(k), device_id_type=MESH)
    for dy, dz in FAR_FIRST:
        pl.semaphore_signal(
            barrier, inc=1, device_id=proto_peer(dy, dz), device_id_type=MESH
        )

    wait_bytes(index_v, in_sem.at[0])
    for i in range(4):
        places = lax.broadcasted_iota(jnp.int32, (256, 128), 0)
        onehot[i] = jnp.where(places == index_v[i : i + 1, :], 1.0, 0.0).astype(BF16)

    def masked(patches, i):
        rows = lax.dot_general(
            onehot[i], patches[256 * i : 256 * i + 256, :],
            (((0,), (0,)), ((), ())), preferred_element_type=F32,
        )
        norm = jnp.sqrt(jnp.sum(rows * rows, axis=1, keepdims=True) + epsilon)
        return rows / norm, norm

    wait_bytes(teacher_v, in_sem.at[1])
    for i in range(4):
        unit, _ = masked(teacher_v, i)
        t_send[128 * i : 128 * i + 128, :] = unit
        t_cast[128 * i : 128 * i + 128, :] = unit.astype(BF16)

    def put_cols(buf, slot, j, sums):
        for q in range(W // 128):
            buf[slot, pl.ds(4 * j + q, 1), :] = sums[:, 128 * q : 128 * q + 128]

    wait_bytes(protos_v, in_sem.at[2])

    def front(j, carry):
        cols = pl.ds(pl.multiple_of(j * W, W), W)
        weights = protos_v[:, cols].astype(F32)
        inv = 1.0 / jnp.sqrt(jnp.sum(weights * weights, axis=0, keepdims=True) + epsilon)
        pinv[:, cols] = inv
        high, low = split(weights * inv)
        pc[:, cols] = high
        plo[:, cols] = low
        block = jnp.exp2(dot(t_cast[...], high) * teacher_scale)
        expos[:, cols] = block
        put_cols(cbuf.at[0], dp, j, jnp.sum(block, axis=0, keepdims=True))
        return carry

    lax.fori_loop(0, 8, front, 0, unroll=2)
    pl.semaphore_wait(barrier, 7 + len(FAR_FIRST))

    def send_cols(t):
        for k in (4, 3, 5, 2, 6, 1, 7):
            remote(cbuf.at[t, dp], cbuf.at[t, dp], c_ssem.at[t], c_rsem.at[t], dp_peer(k)).start()

    def take_cols(t):
        wait_bytes(cbuf.at[t, pl.ds(0, 7)], c_rsem.at[t])
        vrow[...] = 1.0 / jnp.sum(cbuf[t], axis=0)

    def send_rows(buf, t):
        for dy, dz in FAR_FIRST:
            remote(buf.at[pr], buf.at[pr], r_ssem.at[t], r_rsem.at[t], proto_peer(dy, dz)).start()

    def take_rows(buf, t):
        wait_bytes(buf.at[pl.ds(0, 31)], r_rsem.at[t])
        return jnp.sum(buf[...], axis=0)

    def spread(row):
        return jnp.transpose(jnp.broadcast_to(row, (128, 128)))

    def row_pass(buf):
        for i in range(4):
            rows = slice(128 * i, 128 * i + 128)
            total = expos[rows, 0:128] * vrow[0:1, :]
            for k in range(1, 32):
                total += expos[rows, 128 * k : 128 * k + 128] * vrow[k : k + 1, :]
            buf[pr, i : i + 1, :] = jnp.sum(jnp.transpose(total), axis=0, keepdims=True)

    def col_pass(t):
        def chunk(j, carry):
            cols = pl.ds(pl.multiple_of(j * 1024, 1024), 1024)
            sums = jnp.zeros((8, 1024), F32)
            for i in range(64):
                scale = ub[8 * i : 8 * i + 8, :]
                sums += expos[8 * i : 8 * i + 8, cols] * jnp.concatenate([scale] * 8, axis=1)
            total = jnp.sum(sums, axis=0, keepdims=True)
            for q in range(8):
                cbuf[t, dp, pl.ds(8 * j + q, 1), :] = total[:, 128 * q : 128 * q + 128]
            return carry

        lax.fori_loop(0, 4, chunk, 0)

    def spread_rows(values, target):
        for i in range(4):
            target[128 * i : 128 * i + 128, :] = spread(values[i : i + 1, :])

    send_cols(0)
    wait_bytes(student_v, in_sem.at[3])
    for i in range(4):
        unit, norm = masked(student_v, i)
        rows = slice(128 * i, 128 * i + 128)
        s_send[rows, :] = unit
        s_cast[rows, :] = unit.astype(BF16)
        s_inv[rows, :] = jnp.broadcast_to(1.0 / norm, (128, 128))
        s_unit_t[:, rows] = jnp.transpose(unit)
    ts = [
        remote(t_send, t_other, ts_ssem.at[0], ts_rsem.at[0], partner),
        remote(s_send, s_other, ts_ssem.at[1], ts_rsem.at[1], partner),
    ]
    for copy in ts:
        copy.start()

    half = core * 2048
    tot_acc[...] = jnp.zeros_like(tot_acc)
    fp[...] = jnp.zeros_like(fp)

    def student_cols(j, keep):
        at = lax.rem(j * W + half, 4096)
        cols = pl.ds(pl.multiple_of(at, W), W)
        block = jnp.exp2(dot(s_cast[...], pc[:, cols]) * student_scale)
        for q in range(W // 128):
            tot_acc[...] += block[:, 128 * q : 128 * q + 128]
        high, low = split(block)
        if keep:
            mine = pl.ds(pl.multiple_of(j * W, W), W)
            x2h[0:512, mine] = high
            x2l[0:512, mine] = low
        fp[...] += (
            dot_cols(high, pc[:, cols]) + dot_cols(low, pc[:, cols]) + dot_cols(high, plo[:, cols])
        )

    def student_mine(j, carry):
        student_cols(j, True)
        return carry

    def student_rest(j, carry):
        student_cols(j, False)
        return carry

    lax.fori_loop(0, 4, student_mine, 0)
    take_cols(0)
    row_pass(r1buf)
    send_rows(r1buf, 0)

    lax.fori_loop(4, 8, student_rest, 0)
    for i in range(4):
        tbuf[pr, i : i + 1, :] = jnp.sum(
            jnp.transpose(tot_acc[128 * i : 128 * i + 128, :]), axis=0, keepdims=True
        )
    send_rows(tbuf, 3)
    for copy in ts:
        copy.wait_recv()
    t_cast[...] = t_other[...].astype(BF16)
    s_cast[...] = s_other[...].astype(BF16)

    def other_cols(j, carry):
        cols = pl.ds(pl.multiple_of(j * W + half, W), W)
        mine = pl.ds(pl.multiple_of(j * W, W), W)
        high, low = split(jnp.exp2(dot(t_cast[...], pc[:, cols]) * teacher_scale))
        e2h[512:1024, mine] = high
        e2l[512:1024, mine] = low
        high, low = split(jnp.exp2(dot(s_cast[...], pc[:, cols]) * student_scale))
        x2h[512:1024, mine] = high
        x2l[512:1024, mine] = low
        return carry

    lax.fori_loop(0, 4, other_cols, 0)
    spread_rows(1.0 / take_rows(r1buf, 0), ub)
    col_pass(1)

    def send_y(q, src, steps):
        for dy in steps:
            ty = lax.rem(y + dy, NY)
            remote(
                src.at[pl.ds(pl.multiple_of(ty * 128, 128), 128)], yr.at[q, dy - 1],
                y_ssem.at[q], y_rsem.at[q], proto_peer(dy, 0),
            ).start()

    def take_y(q, src):
        wait_bytes(yr.at[q], y_rsem.at[q])
        own = pl.ds(pl.multiple_of(y * 128, 128), 128)
        ysum[q] = src[own, :] + yr[q, 0] + yr[q, 1] + yr[q, 2]

    def send_z(q):
        for dz in (4, 3, 5, 2, 6, 1, 7):
            tz = lax.rem(z + dz, NZ)
            remote(
                ysum.at[q, pl.ds(pl.multiple_of(tz * 16, 16), 16)], zr.at[q, dz - 1],
                z_ssem.at[q], z_rsem.at[q], proto_peer(0, dz),
            ).start()

    def take_z(q):
        wait_bytes(zr.at[q], z_rsem.at[q])
        total = ysum[q, pl.ds(pl.multiple_of(z * 16, 16), 16), :]
        for k in range(7):
            total += zr[q, k]
        return total

    send_cols(1)
    send_y(0, fp, (2,))
    take_cols(1)
    row_pass(r2buf)
    send_rows(r2buf, 1)

    def scale_half(at, ref):
        for i in range(4):
            cols = slice(at + 128 * i, at + 128 * i + 128)
            high, low = split(s_unit_t[:, cols] * ref[i : i + 1, :])
            a_hi[:, cols] = high
            a_lo[:, cols] = low

    def weigh(high, low, cols):
        return (
            dot(a_hi[...], high[:, cols]) + dot(a_lo[...], high[:, cols]) + dot(a_hi[...], low[:, cols])
        )

    tot_row[...] = 1.0 / take_rows(tbuf, 3)
    swap_s[0] = tot_row[...]
    swap_tot = remote(swap_s.at[0], swap_r.at[0], swap_ssem.at[0], swap_rsem.at[0], partner)
    swap_tot.start()
    spread_rows(tot_row[...], totb)
    def own_split(j, carry):
        cols = pl.ds(pl.multiple_of(j * W + half, W), W)
        mine = pl.ds(pl.multiple_of(j * W, W), W)
        high, low = split(expos[:, cols])
        e2h[0:512, mine] = high
        e2l[0:512, mine] = low
        return carry

    lax.fori_loop(0, 4, own_split, 0)
    for i in range(4):
        s_unit_t[:, 512 + 128 * i : 640 + 128 * i] = jnp.transpose(
            s_other[128 * i : 128 * i + 128, :]
        )
    scale_half(0, tot_row)
    swap_tot.wait_recv()
    scale_half(512, swap_r.at[0])

    def probs_part(j, carry):
        mine = pl.ds(pl.multiple_of(j * W, W), W)
        wtp[:, mine] = weigh(x2h, x2l, mine)
        return carry

    lax.fori_loop(0, 4, probs_part, 0)
    spread_rows(1.0 / take_rows(r2buf, 1), ub)
    col_pass(2)

    send_cols(2)
    send_y(0, fp, (1, 3))
    take_cols(2)
    row_pass(r3buf)
    send_rows(r3buf, 2)

    ft[...] = jnp.zeros_like(ft)

    def target_cols(j, carry):
        cols = pl.ds(pl.multiple_of(j * W, W), W)
        unit = pc[:, cols].astype(F32) + plo[:, cols].astype(F32)
        scaled = jnp.concatenate(
            [
                unit[:, 128 * q : 128 * q + 128] * vrow[pl.ds(4 * j + q, 1), :]
                for q in range(W // 128)
            ],
            axis=1,
        )
        b_high, b_low = split(scaled)
        high, low = split(expos[:, cols])
        ft[...] += dot_cols(high, b_high) + dot_cols(low, b_high) + dot_cols(high, b_low)
        return carry

    lax.fori_loop(0, 8, target_cols, 0)
    take_y(0, fp)
    send_z(0)
    send_y(1, ft, (2, 1, 3))
    swap_s[1] = 1.0 / take_rows(r3buf, 2)
    swap_u = remote(swap_s.at[1], swap_r.at[1], swap_ssem.at[1], swap_rsem.at[1], partner)
    swap_u.start()
    def block(d, offset, size):
        return pl.ds(pl.multiple_of(d * 64 + offset, 32), size)

    def protos_part(j, target):
        mine = pl.ds(pl.multiple_of(j * V, V), V)
        cols = pl.ds(pl.multiple_of(j * V + half, V), V)
        at = half // 128 + V // 128 * j
        target = jnp.concatenate(
            [
                target[:, 128 * q : 128 * q + 128] * vrow[pl.ds(at + q, 1), :]
                for q in range(V // 128)
            ],
            axis=1,
        )
        total = wtp[:, mine] - target
        unit = pc[:, cols].astype(F32) + plo[:, cols].astype(F32)
        inner = jnp.sum(unit * total, axis=0, keepdims=True)
        gpart[j] = (total - unit * inner) * (pinv[:, cols] * slope_scale)
        remote(gpart.at[j, block(x_far, 0, 32)], p1r.at[j, 0], p1_ssem.at[j, 0], p1_rsem.at[j, 0], right).start()
        remote(gpart.at[j, block(x_far, 32, 32)], p1r.at[j, 1], p1_ssem.at[j, 1], p1_rsem.at[j, 1], left).start()

    def weigh_some(rows, cols):
        return (
            dot(a_hi[:, rows], e2h[rows, cols])
            + dot(a_lo[:, rows], e2h[rows, cols])
            + dot(a_hi[:, rows], e2l[rows, cols])
        )

    first = pl.ds(0, V)
    scale_half(0, swap_s.at[1])
    target = weigh_some(slice(0, 512), first)
    swap_u.wait_recv()
    scale_half(512, swap_r.at[1])
    protos_part(0, target + weigh_some(slice(512, 1024), first))

    def protos_rest(j, carry):
        protos_part(j, weigh(e2h, e2l, pl.ds(pl.multiple_of(j * V, V), V)))
        return carry

    lax.fori_loop(1, 8, protos_rest, 0)

    def pass_on(j, carry):
        wait_bytes(p1r.at[j, 0], p1_rsem.at[j, 0])
        gpart[j, block(x_next, 0, 32), :] += p1r[j, 0]
        remote(gpart.at[j, block(x_next, 0, 64)], p2r.at[j, 0], p2_ssem.at[j, 0], p2_rsem.at[j, 0], right).start()
        wait_bytes(p1r.at[j, 1], p1_rsem.at[j, 1])
        gpart[j, block(x_prev, 32, 32), :] += p1r[j, 1]
        remote(gpart.at[j, block(x_prev, 0, 64)], p2r.at[j, 1], p2_ssem.at[j, 1], p2_rsem.at[j, 1], left).start()
        return carry

    lax.fori_loop(0, 3, pass_on, 0)
    take_y(1, ft)
    send_z(1)
    lax.fori_loop(3, 8, pass_on, 0)
    spread_rows(swap_s[1], ub)

    own16 = pl.ds(pl.multiple_of(y * 128 + z * 16, 16), 16)
    by_probs = take_z(0)
    by_target = take_z(1)
    unit = s_send[own16, :]
    scale_p = jnp.concatenate([totb[own16, :]] * 2, axis=1)
    scale_t = jnp.concatenate([ub[own16, :]] * 2, axis=1)
    grad = slope_scale * (by_probs * scale_p - by_target * scale_t)
    inner = jnp.sum(unit * grad, axis=1, keepdims=True)
    ag[y, z] = (grad - unit * inner) * jnp.concatenate([s_inv[own16, :]] * 2, axis=1)
    for dz in (4, 3, 5, 2, 6, 1, 7):
        remote(ag.at[y, z], ag.at[y, z], agz_ssem.at[dz - 1], agz_rsem.at[dz - 1], proto_peer(0, dz)).start()

    def to_y(piece):
        for dy in (2, 1, 3):
            remote(piece, piece, agy_ssem, agy_rsem, proto_peer(dy, 0)).start()

    to_y(ag.at[y, z])

    def finish(j, carry):
        wait_bytes(p2r.at[j, 0], p2_rsem.at[j, 0])
        wait_bytes(p2r.at[j, 1], p2_rsem.at[j, 1])

        def rows_of(c):
            at = pl.multiple_of(c * 32, 32)
            return (
                gpart[j, block(x, at, 32), :] + p2r[j, 0, pl.ds(at, 32), :] + p2r[j, 1, pl.ds(at, 32), :]
            )

        fin_s[j] = rows_of(1 - core)
        remote(fin_s.at[j], fin_r.at[j], fin_ssem.at[j], fin_rsem.at[j], partner).start()
        gw_ref[j] = rows_of(core)
        at = pl.multiple_of(j * V + half, V)
        pltpu.make_async_copy(gw_ref.at[j], gw_hbm.at[:, pl.ds(at, V)], out_sem.at[0]).start()
        return carry

    lax.fori_loop(0, 2, finish, 0)
    for dz in (1, 7, 2, 6, 3, 5, 4):
        piece = ag.at[y, lax.rem(z + NZ - dz, NZ)]
        wait_bytes(piece, agz_rsem.at[dz - 1])
        to_y(piece)
    lax.fori_loop(2, 8, finish, 0)

    def finish_other(j, carry):
        wait_bytes(fin_r.at[j], fin_rsem.at[j])
        at = pl.multiple_of(j * V + 2048 - half, V)
        pltpu.make_async_copy(fin_r.at[j], gw_hbm.at[:, pl.ds(at, V)], out_sem.at[0]).start()
        return carry

    lax.fori_loop(0, 8, finish_other, 0)
    wait_bytes(ag.at[pl.ds(0, 3)], agy_rsem)
    rows_out = pltpu.make_async_copy(ag, rows_hbm, out_sem.at[1])
    rows_out.start()

    for t in range(3):
        wait_bytes(cbuf.at[t, pl.ds(0, 7)], c_ssem.at[t])
    for t, buf in enumerate((r1buf, r2buf, r3buf, tbuf)):
        wait_bytes(buf.at[pl.ds(0, 31)], r_ssem.at[t])
    for copy in ts:
        copy.wait_send()
    swap_tot.wait_send()
    swap_u.wait_send()
    for q in range(2):
        wait_bytes(yr.at[q], y_ssem.at[q])
        wait_bytes(zr.at[q], z_ssem.at[q])
    for k in range(7):
        wait_bytes(ag.at[0, 0], agz_ssem.at[k])
    wait_bytes(ag.at[pl.ds(0, 3)], agy_ssem)

    def drain(j, carry):
        for s in range(2):
            wait_bytes(p1r.at[j, s], p1_ssem.at[j, s])
            wait_bytes(p2r.at[j, s], p2_ssem.at[j, s])
        wait_bytes(fin_s.at[j], fin_ssem.at[j])
        return carry

    lax.fori_loop(0, 8, drain, 0)
    wait_bytes(gw_ref, out_sem.at[0])
    wait_bytes(fin_r, out_sem.at[0])
    rows_out.wait()


def place_kernel(rows_hbm, index_ref, gw_in, gp_hbm, gw_hbm, rows, placed, gw, sem, out_sem):
    loads = [pltpu.make_async_copy(rows_hbm.at[i], rows.at[i], sem.at[i]) for i in range(4)]
    gw_load = pltpu.make_async_copy(gw_in, gw, sem.at[4])
    for copy in [*loads, gw_load]:
        copy.start()
    stores = []
    for i in range(4):
        places = lax.broadcasted_iota(jnp.int32, (256, 128), 0)
        onehot = jnp.where(places == index_ref[i : i + 1, :], 1.0, 0.0).astype(BF16)
        loads[i].wait()
        value = rows[i]
        high, low = split(value)
        rest = (value - high.astype(F32) - low.astype(F32)).astype(BF16)
        placed[i] = dot(onehot, high) + dot(onehot, low) + dot(onehot, rest)
        stores.append(
            pltpu.make_async_copy(placed.at[i], gp_hbm.at[pl.ds(256 * i, 256)], out_sem.at[i])
        )
        stores[-1].start()
        if i == 1:
            gw_load.wait()
            stores.append(pltpu.make_async_copy(gw, gw_hbm, out_sem.at[4]))
            stores[-1].start()
    for copy in stores:
        copy.wait()


def body(student_patches, teacher_patches, masked_index, prototypes):
    dma = pltpu.SemaphoreType.DMA

    def vmem(*shape, dtype=F32):
        return pltpu.VMEM(shape, dtype)

    def half_vmem(*shape):
        return pltpu.VMEM(shape, BF16)

    scratch = [
        half_vmem(1024, 256), half_vmem(1024, 256), vmem(4, 128, dtype=jnp.int32), half_vmem(256, 4096), dma((4,)),
        half_vmem(4, 256, 128), vmem(512, 256), vmem(512, 256), vmem(512, 256), vmem(512, 256),
        half_vmem(512, 256), half_vmem(512, 256), vmem(256, 1024), vmem(512, 128),
        half_vmem(256, 4096), half_vmem(256, 4096), vmem(1, 4096), vmem(512, 4096),
        half_vmem(1024, 2048), half_vmem(1024, 2048), half_vmem(1024, 2048), half_vmem(1024, 2048),
        vmem(256, 2048), half_vmem(256, 1024), half_vmem(256, 1024),
        vmem(3, 8, 32, 128), dma((3,)), dma((3,)),
        vmem(32, 4, 128), vmem(32, 4, 128), vmem(32, 4, 128), vmem(32, 4, 128), dma((4,)), dma((4,)),
        vmem(512, 128), vmem(32, 128), vmem(4, 128), vmem(512, 128), vmem(512, 128),
        dma((2,)), dma((2,)), vmem(2, 4, 128), vmem(2, 4, 128), dma((2,)), dma((2,)),
        vmem(512, 256), vmem(512, 256), vmem(2, 3, 128, 256), vmem(2, 128, 256), dma((2,)), dma((2,)),
        vmem(2, 7, 16, 256), dma((2,)), dma((2,)),
        vmem(4, 8, 16, 256), dma((7,)), dma((7,)), dma, dma,
        vmem(8, 256, 256), vmem(8, 2, 32, 256), dma((8, 2)), dma((8, 2)),
        vmem(8, 2, 64, 256), dma((8, 2)), dma((8, 2)),
        vmem(8, 32, 256), vmem(8, 32, 256), dma((8,)), dma((8,)), vmem(8, 32, 256), dma((2,)),
    ]
    anywhere = pl.BlockSpec(memory_space=pl.ANY)
    rows, grad_prototypes = pl.pallas_call(
        kernel,
        out_shape=(
            jax.ShapeDtypeStruct((4, 8, 16, 256), F32),
            jax.ShapeDtypeStruct((32, 4096), F32),
        ),
        in_specs=[anywhere] * 4,
        out_specs=(anywhere, anywhere),
        scratch_shapes=scratch,
        compiler_params=pltpu.CompilerParams(
            collective_id=0, has_side_effects=True, vmem_limit_bytes=60 * 1024 * 1024
        ),
    )(student_patches, teacher_patches, masked_index, prototypes)
    return pl.pallas_call(
        place_kernel,
        out_shape=(
            jax.ShapeDtypeStruct((1024, 256), F32),
            jax.ShapeDtypeStruct((32, 4096), F32),
        ),
        in_specs=[anywhere, pl.BlockSpec(memory_space=pltpu.VMEM), anywhere],
        out_specs=(anywhere, anywhere),
        scratch_shapes=[vmem(4, 128, 256), vmem(4, 256, 256), vmem(32, 4096), dma((5,)), dma((5,))],
    )(rows.reshape(4, 128, 256), masked_index, grad_prototypes)


def solution(mesh):
    placed = (P("dp", None), P("dp", None), P("dp", None), P(None, "proto"))
    return jax.shard_map(
        body,
        mesh=mesh,
        in_specs=placed,
        out_specs=(P("dp", None), P("dp", "proto")),
        check_vma=False,
    )
```

```python
import math

import jax
import jax.numpy as jnp
from jax import lax
from jax.experimental import pallas as pl
from jax.experimental.pallas import tpu as pltpu
from jax.sharding import PartitionSpec as P

MESH = pl.DeviceIdType.MESH
F32 = jnp.float32
BF16 = jnp.bfloat16

teacher_scale = math.log2(math.e) / 0.07
student_scale = math.log2(math.e) / 0.1
slope_scale = 4096.0 / 0.1
epsilon = 1e-06

W = 512
V = 256
NY, NZ = 4, 8
Z_FAR_FIRST = (4, 3, 5, 2, 6, 1, 7, 0)
FAR_FIRST = sorted(
    [(dy, dz) for dy in range(NY) for dz in range(NZ) if dy or dz],
    key=lambda o: -(min(o[0], NY - o[0]) + min(o[1], NZ - o[1])),
)


def dot(a, b):
    return jnp.dot(a, b, preferred_element_type=F32)


def dot_cols(a, b):
    return lax.dot_general(a, b, (((1,), (1,)), ((), ())), preferred_element_type=F32)


def split(value):
    high = value.astype(BF16)
    return high, (value - high.astype(F32)).astype(BF16)


def kernel(
    student_hbm, teacher_hbm, index_hbm, protos_hbm,
    rows_hbm, gw_hbm,
    student_v, teacher_v, index_v, protos_v, in_sem, protos_sem,
    onehot, t_send, s_send, t_other, s_other, t_cast, s_cast, s_unit_t, s_inv,
    pc, plo, pinv, expos,
    e2h, e2l, x2h, x2l, wtp, a_hi, a_lo,
    cbuf, c_ssem, c_rsem,
    rbuf, r_ssem, r_rsem, ub, row_acc, vrow, tot_row, tot_acc, totb,
    ts_ssem, ts_rsem, swap_s, swap_r, swap_ssem, swap_rsem,
    fp, ft, yr, ysum, y_ssem, y_rsem, yp_ssem, yp_rsem, zr, z_ssem, z_rsem,
    ag, agz_ssem, agz_rsem, agy_ssem, agy_rsem,
    gpart, p1r, p1_ssem, p1_rsem, p2r, p2_ssem, p2_rsem,
    gw_ref, out_sem,
):
    dp = lax.axis_index("dp")
    pr = lax.axis_index("proto")
    x, core = lax.div(dp, 2), lax.rem(dp, 2)
    y, z = lax.div(pr, NZ), lax.rem(pr, NZ)
    x_next, x_prev, x_far = lax.rem(x + 1, 4), lax.rem(x + 3, 4), lax.rem(x + 2, 4)
    right = (x_next * 2 + core, pr)
    left = (x_prev * 2 + core, pr)
    partner = (x * 2 + 1 - core, pr)

    def dp_peer(k):
        return (lax.rem(dp + k, 8), pr)

    def proto_peer(dy, dz):
        return (dp, lax.rem(y + dy, NY) * NZ + lax.rem(z + dz, NZ))

    def remote(src, dst, ssem, rsem, device):
        return pltpu.make_async_remote_copy(
            src, dst, ssem, rsem, device_id=device, device_id_type=MESH
        )

    def wait_bytes(ref, sem):
        pltpu.make_async_copy(ref, ref, sem).wait()

    def load(src, dst, sem, parts):
        size = src.shape[0] // parts
        for i in range(parts):
            rows = pl.ds(i * size, size)
            pltpu.make_async_copy(src.at[rows], dst.at[rows], sem).start()

    load(index_hbm, index_v, in_sem.at[0], 1)
    for j in range(4):
        cols = pl.ds(2 * W * j, 2 * W)
        pltpu.make_async_copy(protos_hbm.at[:, cols], protos_v.at[j], protos_sem.at[j]).start()
        if j == 0:
            load(teacher_hbm, teacher_v, in_sem.at[1], 4)
    load(student_hbm, student_v, in_sem.at[3], 4)
    barrier = pltpu.get_barrier_semaphore()
    for k in range(1, 8):
        pl.semaphore_signal(barrier, inc=1, device_id=dp_peer(k), device_id_type=MESH)
    for dy, dz in FAR_FIRST:
        pl.semaphore_signal(
            barrier, inc=1, device_id=proto_peer(dy, dz), device_id_type=MESH
        )

    wait_bytes(index_v, in_sem.at[0])
    for i in range(4):
        places = lax.broadcasted_iota(jnp.int32, (256, 128), 0)
        onehot[i] = jnp.where(places == index_v[i : i + 1, :], 1.0, 0.0).astype(BF16)

    def masked(patches, i):
        rows = lax.dot_general(
            onehot[i], patches[256 * i : 256 * i + 256, :],
            (((0,), (0,)), ((), ())), preferred_element_type=F32,
        )
        norm = jnp.sqrt(jnp.sum(rows * rows, axis=1, keepdims=True) + epsilon)
        return rows / norm, norm

    def norm_piece(q):
        wait_bytes(protos_v.at[q], protos_sem.at[q])
        for i in range(2):
            cols = pl.ds(pl.multiple_of((2 * q + i) * W, W), W)
            weights = protos_v[q, :, W * i : W * i + W].astype(F32)
            inv = 1.0 / jnp.sqrt(jnp.sum(weights * weights, axis=0, keepdims=True) + epsilon)
            pinv[:, cols] = inv
            pc[:, cols] = (weights * inv).astype(BF16)

    norm_piece(0)
    wait_bytes(teacher_v, in_sem.at[1])
    for i in range(4):
        unit, _ = masked(teacher_v, i)
        t_send[128 * i : 128 * i + 128, :] = unit
        t_cast[128 * i : 128 * i + 128, :] = unit.astype(BF16)

    def put_cols(buf, slot, j, sums):
        for q in range(W // 128):
            buf[slot, pl.ds(4 * j + q, 1), :] = sums[:, 128 * q : 128 * q + 128]


    def send_cols(t, q):
        piece = cbuf.at[t, dp, pl.ds(pl.multiple_of(8 * q, 8), 8)]
        for k in (4, 3, 5, 2, 6, 1, 7):
            remote(piece, piece, c_ssem, c_rsem.at[t, q // 2], dp_peer(k)).start()

    def take_cols(t, h):
        wait_bytes(cbuf.at[t, pl.ds(0, 7), pl.ds(16 * h, 16)], c_rsem.at[t, h])
        rows = slice(16 * h, 16 * h + 16)
        vrow[rows, :] = 1.0 / jnp.sum(cbuf[t, :, rows, :], axis=0)

    def score_piece(q):
        for i in range(2):
            j = 2 * q + i
            cols = pl.ds(pl.multiple_of(j * W, W), W)
            block = jnp.exp2(dot(t_cast[...], pc[:, cols]) * teacher_scale)
            expos[:, cols] = block
            put_cols(cbuf.at[0], dp, j, jnp.sum(block, axis=0, keepdims=True))

    def front(q, carry):
        norm_piece(q + 1)
        score_piece(q)
        return carry

    def low_part(q, carry):
        for i in range(2):
            cols = pl.ds(pl.multiple_of((2 * q + i) * W, W), W)
            unit = protos_v[q, :, W * i : W * i + W].astype(F32) * pinv[:, cols]
            plo[:, cols] = (unit - pc[:, cols].astype(F32)).astype(BF16)
        return carry

    lax.fori_loop(0, 3, front, 0)
    score_piece(3)
    pl.semaphore_wait(barrier, 7 + len(FAR_FIRST))
    for q in range(4):
        send_cols(0, q)

    def send_rows(t):
        for dy, dz in FAR_FIRST:
            remote(rbuf.at[t, pr], rbuf.at[t, pr], r_ssem, r_rsem.at[t], proto_peer(dy, dz)).start()

    def take_rows(t):
        wait_bytes(rbuf.at[t, pl.ds(0, 31)], r_rsem.at[t])
        return jnp.sum(rbuf[t], axis=0)

    def spread(row):
        return jnp.transpose(jnp.broadcast_to(row, (128, 128)))

    def row_pass(t):
        take_cols(t, 0)
        for i in range(4):
            rows = slice(128 * i, 128 * i + 128)
            total = expos[rows, 0:128] * vrow[0:1, :]
            for k in range(1, 16):
                total += expos[rows, 128 * k : 128 * k + 128] * vrow[k : k + 1, :]
            row_acc[rows, :] = total
        take_cols(t, 1)
        for i in range(4):
            rows = slice(128 * i, 128 * i + 128)
            total = row_acc[rows, :]
            for k in range(16, 32):
                total += expos[rows, 128 * k : 128 * k + 128] * vrow[k : k + 1, :]
            rbuf[t, pr, i : i + 1, :] = jnp.sum(jnp.transpose(total), axis=0, keepdims=True)

    def col_pass(t):
        def chunk(j, carry):
            cols = pl.ds(pl.multiple_of(j * 1024, 1024), 1024)
            sums = jnp.zeros((8, 1024), F32)
            for i in range(64):
                scale = ub[8 * i : 8 * i + 8, :]
                sums += expos[8 * i : 8 * i + 8, cols] * jnp.concatenate([scale] * 8, axis=1)
            total = jnp.sum(sums, axis=0, keepdims=True)
            for q in range(8):
                cbuf[t, dp, pl.ds(8 * j + q, 1), :] = total[:, 128 * q : 128 * q + 128]
            send_cols(t, j)
            return carry

        lax.fori_loop(0, 4, chunk, 0)

    def spread_rows(values, target):
        for i in range(4):
            target[128 * i : 128 * i + 128, :] = spread(values[i : i + 1, :])

    wait_bytes(student_v, in_sem.at[3])
    for i in range(4):
        unit, norm = masked(student_v, i)
        rows = slice(128 * i, 128 * i + 128)
        s_send[rows, :] = unit
        s_cast[rows, :] = unit.astype(BF16)
        s_inv[rows, :] = jnp.broadcast_to(1.0 / norm, (128, 128))
        s_unit_t[:, rows] = jnp.transpose(unit)
    ts = [
        remote(t_send, t_other, ts_ssem.at[0], ts_rsem.at[0], partner),
        remote(s_send, s_other, ts_ssem.at[1], ts_rsem.at[1], partner),
    ]
    for copy in ts:
        copy.start()

    half = core * 2048
    tot_acc[...] = jnp.zeros_like(tot_acc)
    fp[...] = jnp.zeros_like(fp)

    def student_cols(j, keep):
        at = lax.rem(j * W + half, 4096)
        cols = pl.ds(pl.multiple_of(at, W), W)
        block = jnp.exp2(dot(s_cast[...], pc[:, cols]) * student_scale)
        for q in range(W // 128):
            tot_acc[...] += block[:, 128 * q : 128 * q + 128]
        high, low = split(block)
        if keep:
            mine = pl.ds(pl.multiple_of(j * W, W), W)
            x2h[0:512, mine] = high
            x2l[0:512, mine] = low
        fp[...] += (
            dot_cols(high, pc[:, cols]) + dot_cols(low, pc[:, cols]) + dot_cols(high, plo[:, cols])
        )

    def student_mine(j, carry):
        student_cols(j, True)
        return carry

    def student_rest(j, carry):
        student_cols(j, False)
        return carry

    lax.fori_loop(0, 4, low_part, 0)
    lax.fori_loop(0, 2, student_mine, 0)
    row_pass(0)
    send_rows(0)

    lax.fori_loop(2, 4, student_mine, 0)
    lax.fori_loop(4, 8, student_rest, 0)
    for i in range(4):
        rbuf[3, pr, i : i + 1, :] = jnp.sum(
            jnp.transpose(tot_acc[128 * i : 128 * i + 128, :]), axis=0, keepdims=True
        )
    send_rows(3)
    spread_rows(1.0 / take_rows(0), ub)
    col_pass(1)

    def send_y(q, src, steps):
        for dy in steps:
            ty = lax.rem(y + dy, NY)
            remote(
                src.at[pl.ds(pl.multiple_of(ty * 128, 128), 128)], yr.at[q, dy - 1],
                y_ssem.at[q], y_rsem.at[q], proto_peer(dy, 0),
            ).start()

    def take_y(q, src):
        wait_bytes(yr.at[q], y_rsem.at[q])
        own = pl.ds(pl.multiple_of(y * 128, 128), 128)
        ysum[q] = src[own, :] + yr[q, 0] + yr[q, 1] + yr[q, 2]

    def send_z(q):
        for dz in (4, 3, 5, 2, 6, 1, 7):
            tz = lax.rem(z + dz, NZ)
            remote(
                ysum.at[q, pl.ds(pl.multiple_of(tz * 16, 16), 16)], zr.at[q, dz - 1],
                z_ssem, z_rsem.at[q], proto_peer(0, dz),
            ).start()

    def take_z(q):
        wait_bytes(zr.at[q], z_rsem.at[q])
        total = ysum[q, pl.ds(pl.multiple_of(z * 16, 16), 16), :]
        for k in range(7):
            total += zr[q, k]
        return total

    send_y(0, fp, (2,))
    for copy in ts:
        copy.wait_recv()
    t_cast[...] = t_other[...].astype(BF16)
    s_cast[...] = s_other[...].astype(BF16)

    def other_cols(j, carry):
        cols = pl.ds(pl.multiple_of(j * W + half, W), W)
        mine = pl.ds(pl.multiple_of(j * W, W), W)
        high, low = split(jnp.exp2(dot(t_cast[...], pc[:, cols]) * teacher_scale))
        e2h[512:1024, mine] = high
        e2l[512:1024, mine] = low
        high, low = split(jnp.exp2(dot(s_cast[...], pc[:, cols]) * student_scale))
        x2h[512:1024, mine] = high
        x2l[512:1024, mine] = low
        return carry

    lax.fori_loop(0, 4, other_cols, 0)
    row_pass(1)
    send_rows(1)

    def scale_half(at, ref):
        for i in range(4):
            cols = slice(at + 128 * i, at + 128 * i + 128)
            high, low = split(s_unit_t[:, cols] * ref[i : i + 1, :])
            a_hi[:, cols] = high
            a_lo[:, cols] = low

    def weigh(high, low, cols):
        return (
            dot(a_hi[...], high[:, cols]) + dot(a_lo[...], high[:, cols]) + dot(a_hi[...], low[:, cols])
        )

    tot_row[...] = 1.0 / take_rows(3)
    swap_s[0] = tot_row[...]
    swap_tot = remote(swap_s.at[0], swap_r.at[0], swap_ssem.at[0], swap_rsem.at[0], partner)
    swap_tot.start()
    spread_rows(tot_row[...], totb)
    def own_split(j, carry):
        cols = pl.ds(pl.multiple_of(j * W + half, W), W)
        mine = pl.ds(pl.multiple_of(j * W, W), W)
        high, low = split(expos[:, cols])
        e2h[0:512, mine] = high
        e2l[0:512, mine] = low
        return carry

    lax.fori_loop(0, 4, own_split, 0)
    for i in range(4):
        s_unit_t[:, 512 + 128 * i : 640 + 128 * i] = jnp.transpose(
            s_other[128 * i : 128 * i + 128, :]
        )
    scale_half(0, tot_row)
    swap_tot.wait_recv()
    scale_half(512, swap_r.at[0])

    def probs_part(j, carry):
        mine = pl.ds(pl.multiple_of(j * W, W), W)
        wtp[:, mine] = weigh(x2h, x2l, mine)
        return carry

    lax.fori_loop(0, 4, probs_part, 0)
    spread_rows(1.0 / take_rows(1), ub)
    col_pass(2)

    send_y(0, fp, (1, 3))
    row_pass(2)
    send_rows(2)

    ft[...] = jnp.zeros_like(ft)

    def target_cols(j, carry):
        cols = pl.ds(pl.multiple_of(j * W, W), W)
        unit = pc[:, cols].astype(F32) + plo[:, cols].astype(F32)
        scaled = jnp.concatenate(
            [
                unit[:, 128 * q : 128 * q + 128] * vrow[pl.ds(4 * j + q, 1), :]
                for q in range(W // 128)
            ],
            axis=1,
        )
        b_high, b_low = split(scaled)
        high, low = split(expos[:, cols])
        ft[...] += dot_cols(high, b_high) + dot_cols(low, b_high) + dot_cols(high, b_low)
        return carry

    lax.fori_loop(0, 4, target_cols, 0, unroll=2)
    take_y(0, fp)
    send_z(0)
    lax.fori_loop(4, 8, target_cols, 0, unroll=2)
    for n, dz in enumerate(Z_FAR_FIRST):
        tz = lax.rem(z + dz, NZ) * 16
        for dy in (2, 1, 3):
            ty = lax.rem(y + dy, NY) * 128
            remote(
                ft.at[pl.ds(pl.multiple_of(ty + tz, 16), 16)], yr.at[1, dy - 1, pl.ds(pl.multiple_of(tz, 16), 16)],
                yp_ssem, yp_rsem.at[n // 4], proto_peer(dy, 0),
            ).start()
    swap_s[1] = 1.0 / take_rows(2)
    swap_u = remote(swap_s.at[1], swap_r.at[1], swap_ssem.at[1], swap_rsem.at[1], partner)
    swap_u.start()
    def block(d, offset, size):
        return pl.ds(pl.multiple_of(d * 64 + offset, 32), size)

    def protos_part(j, target):
        mine = pl.ds(pl.multiple_of(j * V, V), V)
        cols = pl.ds(pl.multiple_of(j * V + half, V), V)
        at = half // 128 + V // 128 * j
        target = jnp.concatenate(
            [
                target[:, 128 * q : 128 * q + 128] * vrow[pl.ds(at + q, 1), :]
                for q in range(V // 128)
            ],
            axis=1,
        )
        total = wtp[:, mine] - target
        unit = pc[:, cols].astype(F32) + plo[:, cols].astype(F32)
        inner = jnp.sum(unit * total, axis=0, keepdims=True)
        gpart[j] = (total - unit * inner) * (pinv[:, cols] * slope_scale)
        remote(gpart.at[j, block(x_far, 0, 32)], p1r.at[j, 0], p1_ssem, p1_rsem.at[j], right).start()
        remote(gpart.at[j, block(x_far, 32, 32)], p1r.at[j, 1], p1_ssem, p1_rsem.at[j], left).start()
        remote(gpart.at[j, block(x, 32 - 32 * core, 32)], p2r.at[j, 4], p2_ssem, p2_rsem.at[j], partner).start()

    def weigh_some(rows, cols):
        return (
            dot(a_hi[:, rows], e2h[rows, cols])
            + dot(a_lo[:, rows], e2h[rows, cols])
            + dot(a_hi[:, rows], e2l[rows, cols])
        )

    first = pl.ds(0, V)
    scale_half(0, swap_s.at[1])
    target = weigh_some(slice(0, 512), first)
    swap_u.wait_recv()
    scale_half(512, swap_r.at[1])
    protos_part(0, target + weigh_some(slice(512, 1024), first))

    def protos_rest(j, carry):
        protos_part(j, weigh(e2h, e2l, pl.ds(pl.multiple_of(j * V, V), V)))
        return carry

    def take_pieces(first, last):
        wait_bytes(yr.at[1, pl.ds(0, 3), pl.ds(0, 64)], yp_rsem.at[first // 4])
        for dz in Z_FAR_FIRST[first:last]:
            tz = lax.rem(z + dz, NZ) * 16
            rows = pl.ds(pl.multiple_of(tz, 16), 16)
            own = pl.ds(pl.multiple_of(y * 128 + tz, 16), 16)
            ysum[1, rows, :] = ft[own, :] + yr[1, 0, rows, :] + yr[1, 1, rows, :] + yr[1, 2, rows, :]
            if dz:
                remote(
                    ysum.at[1, rows], zr.at[1, dz - 1], z_ssem, z_rsem.at[1], proto_peer(0, dz)
                ).start()

    def pass_on(j, carry):
        wait_bytes(p1r.at[j], p1_rsem.at[j])
        for s, side in enumerate((x_next, x_prev)):
            gpart[j, block(side, 32 * s, 32), :] += p1r[j, s]
            for c in range(2):
                remote(
                    gpart.at[j, block(side, 32 * c, 32)], p2r.at[j, 2 * s + core],
                    p2_ssem, p2_rsem.at[j], (side * 2 + c, pr),
                ).start()
        return carry

    lax.fori_loop(1, 5, protos_rest, 0)
    pass_on(0, 0)
    take_pieces(0, 4)
    lax.fori_loop(5, 8, protos_rest, 0)

    lax.fori_loop(1, 4, pass_on, 0)
    take_pieces(4, 8)
    lax.fori_loop(4, 6, pass_on, 0)
    spread_rows(swap_s[1], ub)

    own16 = pl.ds(pl.multiple_of(y * 128 + z * 16, 16), 16)
    by_probs = take_z(0)
    by_target = take_z(1)
    unit = s_send[own16, :]
    scale_p = jnp.concatenate([totb[own16, :]] * 2, axis=1)
    scale_t = jnp.concatenate([ub[own16, :]] * 2, axis=1)
    grad = slope_scale * (by_probs * scale_p - by_target * scale_t)
    inner = jnp.sum(unit * grad, axis=1, keepdims=True)
    ag[y, z] = (grad - unit * inner) * jnp.concatenate([s_inv[own16, :]] * 2, axis=1)
    for dz in (1, 7, 2, 6, 3, 5, 4):
        remote(ag.at[y, z], ag.at[y, z], agz_ssem, agz_rsem.at[dz - 1], proto_peer(0, dz)).start()

    def to_y(piece):
        for dy in (2, 1, 3):
            remote(piece, piece, agy_ssem, agy_rsem.at[dy - 1], proto_peer(dy, 0)).start()

    to_y(ag.at[y, z])
    lax.fori_loop(6, 8, pass_on, 0)

    def finish(j, carry):
        wait_bytes(p2r.at[j], p2_rsem.at[j])
        gw_ref[j, 0] = gpart[j, block(x, 32 * core, 32), :] + p2r[j, core] + p2r[j, 2 + core]
        gw_ref[j, 1] = p2r[j, 4] + p2r[j, 1 - core] + p2r[j, 3 - core]
        for i, start in enumerate((half, 2048 - half)):
            cols = pl.ds(pl.multiple_of(j * V + start, V), V)
            pltpu.make_async_copy(gw_ref.at[j, i], gw_hbm.at[:, cols], out_sem.at[0]).start()
        return carry

    for dz in (1, 7, 2, 6, 3, 5, 4):
        piece = ag.at[y, lax.rem(z + NZ - dz, NZ)]
        wait_bytes(piece, agz_rsem.at[dz - 1])
        to_y(piece)
    pltpu.make_async_copy(ag.at[y], rows_hbm.at[y], out_sem.at[1]).start()
    lax.fori_loop(0, 8, finish, 0)

    for dy in (1, 3, 2):
        image = lax.rem(y + NY - dy, NY)
        wait_bytes(ag.at[image], agy_rsem.at[dy - 1])
        pltpu.make_async_copy(ag.at[image], rows_hbm.at[image], out_sem.at[1]).start()

    wait_bytes(cbuf.at[:, pl.ds(0, 7)], c_ssem)
    wait_bytes(rbuf.at[:, pl.ds(0, 31)], r_ssem)
    for copy in ts:
        copy.wait_send()
    swap_tot.wait_send()
    swap_u.wait_send()
    wait_bytes(yr.at[0], y_ssem.at[0])
    wait_bytes(yr.at[1], yp_ssem)
    wait_bytes(zr, z_ssem)
    wait_bytes(ag.at[0, pl.ds(0, 7)], agz_ssem)
    wait_bytes(ag.at[pl.ds(0, 3)], agy_ssem)

    wait_bytes(p1r, p1_ssem)
    wait_bytes(p2r, p2_ssem)
    wait_bytes(gw_ref, out_sem.at[0])
    wait_bytes(ag, out_sem.at[1])


def place_kernel(rows_hbm, index_hbm, gw_in, gp_hbm, gw_hbm, rows, index, placed, gw, sem, out_sem):
    gw_load = pltpu.make_async_copy(gw_in, gw, sem.at[5])
    loads = [pltpu.make_async_copy(index_hbm, index, sem.at[4])]
    loads += [pltpu.make_async_copy(rows_hbm.at[i], rows.at[i], sem.at[i]) for i in range(4)]
    for copy in [*loads, gw_load]:
        copy.start()
    loads[0].wait()
    onehots = []
    for i in range(4):
        places = lax.broadcasted_iota(jnp.int32, (256, 128), 0)
        onehots.append(jnp.where(places == index[i : i + 1, :], 1.0, 0.0).astype(BF16))
    for copy in loads[1:]:
        copy.wait()
    stores = []
    for i in range(4):
        value = rows[i]
        high, low = split(value)
        rest = (value - high.astype(F32) - low.astype(F32)).astype(BF16)
        placed[i] = dot(onehots[i], high) + dot(onehots[i], low) + dot(onehots[i], rest)
        stores.append(
            pltpu.make_async_copy(placed.at[i], gp_hbm.at[pl.ds(256 * i, 256)], out_sem.at[i])
        )
        stores[-1].start()
        if i == 0:
            gw_load.wait()
            stores.append(pltpu.make_async_copy(gw, gw_hbm, out_sem.at[4]))
            stores[-1].start()
    for copy in stores:
        copy.wait()


def body(student_patches, teacher_patches, masked_index, prototypes):
    dma = pltpu.SemaphoreType.DMA

    def vmem(*shape, dtype=F32):
        return pltpu.VMEM(shape, dtype)

    def half_vmem(*shape):
        return pltpu.VMEM(shape, BF16)

    scratch = [
        half_vmem(1024, 256), half_vmem(1024, 256), vmem(4, 128, dtype=jnp.int32), half_vmem(4, 256, 1024), dma((4,)), dma((4,)),
        half_vmem(4, 256, 128), vmem(512, 256), vmem(512, 256), vmem(512, 256), vmem(512, 256),
        half_vmem(512, 256), half_vmem(512, 256), vmem(256, 1024), vmem(512, 128),
        half_vmem(256, 4096), half_vmem(256, 4096), vmem(1, 4096), vmem(512, 4096),
        half_vmem(1024, 2048), half_vmem(1024, 2048), half_vmem(1024, 2048), half_vmem(1024, 2048),
        vmem(256, 2048), half_vmem(256, 1024), half_vmem(256, 1024),
        vmem(3, 8, 32, 128), dma, dma((3, 2)),
        vmem(4, 32, 4, 128), dma, dma((4,)),
        vmem(512, 128), vmem(512, 128), vmem(32, 128), vmem(4, 128), vmem(512, 128), vmem(512, 128),
        dma((2,)), dma((2,)), vmem(2, 4, 128), vmem(2, 4, 128), dma((2,)), dma((2,)),
        vmem(512, 256), vmem(512, 256), vmem(2, 3, 128, 256), vmem(2, 128, 256), dma((1,)), dma((1,)), dma, dma((2,)),
        vmem(2, 7, 16, 256), dma, dma((2,)),
        vmem(4, 8, 16, 256), dma, dma((7,)), dma, dma((3,)),
        vmem(8, 256, 256), vmem(8, 2, 32, 256), dma, dma((8,)),
        vmem(8, 5, 32, 256), dma, dma((8,)), vmem(8, 2, 32, 256), dma((2,)),
    ]
    anywhere = pl.BlockSpec(memory_space=pl.ANY)
    rows, grad_prototypes = pl.pallas_call(
        kernel,
        out_shape=(
            jax.ShapeDtypeStruct((4, 8, 16, 256), F32),
            jax.ShapeDtypeStruct((32, 4096), F32),
        ),
        in_specs=[anywhere] * 4,
        out_specs=(anywhere, anywhere),
        scratch_shapes=scratch,
        compiler_params=pltpu.CompilerParams(
            collective_id=0, has_side_effects=True, vmem_limit_bytes=60 * 1024 * 1024
        ),
    )(student_patches, teacher_patches, masked_index, prototypes)
    return pl.pallas_call(
        place_kernel,
        out_shape=(
            jax.ShapeDtypeStruct((1024, 256), F32),
            jax.ShapeDtypeStruct((32, 4096), F32),
        ),
        in_specs=[anywhere] * 3,
        out_specs=(anywhere, anywhere),
        scratch_shapes=[
            vmem(4, 128, 256), vmem(4, 128, dtype=jnp.int32), vmem(4, 256, 256), vmem(32, 4096), dma((6,)), dma((5,)),
        ],
    )(rows.reshape(4, 128, 256), masked_index, grad_prototypes)


def solution(mesh):
    placed = (P("dp", None), P("dp", None), P("dp", None), P(None, "proto"))
    return jax.shard_map(
        body,
        mesh=mesh,
        in_specs=placed,
        out_specs=(P("dp", None), P("dp", "proto")),
        check_vma=False,
    )
```

```python
import math

import jax
import jax.numpy as jnp
from jax import lax
from jax.experimental import pallas as pl
from jax.experimental.pallas import tpu as pltpu
from jax.sharding import PartitionSpec as P

MESH = pl.DeviceIdType.MESH
F32 = jnp.float32
BF16 = jnp.bfloat16

teacher_scale = math.log2(math.e) / 0.07
student_scale = math.log2(math.e) / 0.1
slope_scale = 4096.0 / 0.1
epsilon = 1e-06

W = 512
V = 256
NY, NZ = 4, 8
Z_FAR_FIRST = (4, 3, 5, 2, 6, 1, 7, 0)
FAR_FIRST = sorted(
    [(dy, dz) for dy in range(NY) for dz in range(NZ) if dy or dz],
    key=lambda o: -(min(o[0], NY - o[0]) + min(o[1], NZ - o[1])),
)


def dot(a, b):
    return jnp.dot(a, b, preferred_element_type=F32)


def dot_cols(a, b):
    return lax.dot_general(a, b, (((1,), (1,)), ((), ())), preferred_element_type=F32)


def split(value):
    high = value.astype(BF16)
    return high, (value - high.astype(F32)).astype(BF16)


def kernel(
    student_hbm, teacher_hbm, index_hbm, protos_hbm,
    rows_hbm, gw_hbm,
    student_v, teacher_v, index_v, protos_v, in_sem, protos_sem,
    onehot, t_send, s_send, t_other, s_other, t_cast, s_cast, s_unit_t, s_inv,
    pc, plo, pinv, expos,
    e2h, e2l, x2h, x2l, wtp, a_hi, a_lo,
    cbuf, c_ssem, c_rsem,
    rbuf, r_ssem, r_rsem, ub, row_acc, vrow, tot_row, tot_acc, totb,
    ts_ssem, ts_rsem, swap_s, swap_r, swap_ssem, swap_rsem,
    fp, ft, yr, ysum, y_ssem, y_rsem, yp_ssem, yp_rsem, zr, z_ssem, z_rsem,
    ag, agz_ssem, agz_rsem, agy_ssem, agy_rsem,
    gpart, p1r, p1_ssem, p1_rsem, p2r, p2_ssem, p2_rsem,
    gw_ref, out_sem,
):
    dp = lax.axis_index("dp")
    pr = lax.axis_index("proto")
    x, core = lax.div(dp, 2), lax.rem(dp, 2)
    y, z = lax.div(pr, NZ), lax.rem(pr, NZ)
    x_next, x_prev, x_far = lax.rem(x + 1, 4), lax.rem(x + 3, 4), lax.rem(x + 2, 4)
    right = (x_next * 2 + core, pr)
    left = (x_prev * 2 + core, pr)
    partner = (x * 2 + 1 - core, pr)

    def dp_peer(k):
        return (lax.rem(dp + k, 8), pr)

    def proto_peer(dy, dz):
        return (dp, lax.rem(y + dy, NY) * NZ + lax.rem(z + dz, NZ))

    def remote(src, dst, ssem, rsem, device):
        return pltpu.make_async_remote_copy(
            src, dst, ssem, rsem, device_id=device, device_id_type=MESH
        )

    def wait_bytes(ref, sem):
        pltpu.make_async_copy(ref, ref, sem).wait()

    def load(src, dst, sem, parts):
        size = src.shape[0] // parts
        for i in range(parts):
            rows = pl.ds(i * size, size)
            pltpu.make_async_copy(src.at[rows], dst.at[rows], sem).start()

    load(index_hbm, index_v, in_sem.at[0], 1)
    load(teacher_hbm, teacher_v, in_sem.at[1], 4)
    for j in range(4):
        cols = pl.ds(2 * W * j, 2 * W)
        pltpu.make_async_copy(protos_hbm.at[:, cols], protos_v.at[j], protos_sem.at[j]).start()
    load(student_hbm, student_v, in_sem.at[3], 4)
    barrier = pltpu.get_barrier_semaphore()
    for k in range(1, 8):
        pl.semaphore_signal(barrier, inc=1, device_id=dp_peer(k), device_id_type=MESH)
    for dy, dz in FAR_FIRST:
        pl.semaphore_signal(
            barrier, inc=1, device_id=proto_peer(dy, dz), device_id_type=MESH
        )

    wait_bytes(index_v, in_sem.at[0])
    for i in range(4):
        places = lax.broadcasted_iota(jnp.int32, (256, 128), 0)
        onehot[i] = jnp.where(places == index_v[i : i + 1, :], 1.0, 0.0).astype(BF16)

    def masked(patches, i):
        rows = lax.dot_general(
            onehot[i], patches[256 * i : 256 * i + 256, :],
            (((0,), (0,)), ((), ())), preferred_element_type=F32,
        )
        norm = jnp.sqrt(jnp.sum(rows * rows, axis=1, keepdims=True) + epsilon)
        return rows / norm, norm

    wait_bytes(teacher_v, in_sem.at[1])
    for i in range(4):
        unit, _ = masked(teacher_v, i)
        t_send[128 * i : 128 * i + 128, :] = unit
        t_cast[128 * i : 128 * i + 128, :] = unit.astype(BF16)

    def put_cols(buf, slot, j, sums):
        for q in range(W // 128):
            buf[slot, pl.ds(4 * j + q, 1), :] = sums[:, 128 * q : 128 * q + 128]


    def send_cols(t, q):
        piece = cbuf.at[t, dp, pl.ds(pl.multiple_of(8 * q, 8), 8)]
        for k in (4, 3, 5, 2, 6, 1, 7):
            remote(piece, piece, c_ssem, c_rsem.at[t, q], dp_peer(k)).start()

    def take_cols(t, q):
        rows = slice(8 * q, 8 * q + 8)
        wait_bytes(cbuf.at[t, pl.ds(0, 7), rows], c_rsem.at[t, q])
        vrow[rows, :] = 1.0 / jnp.sum(cbuf[t, :, rows, :], axis=0)

    def front(q, carry):
        wait_bytes(protos_v.at[q], protos_sem.at[q])
        for i in range(2):
            j = 2 * q + i
            cols = pl.ds(pl.multiple_of(j * W, W), W)
            weights = protos_v[q, :, W * i : W * i + W].astype(F32)
            inv = 1.0 / jnp.sqrt(jnp.sum(weights * weights, axis=0, keepdims=True) + epsilon)
            pinv[:, cols] = inv
            unit = (weights * inv).astype(BF16)
            pc[:, cols] = unit
            block = jnp.exp2(dot(t_cast[...], unit) * teacher_scale)
            expos[:, cols] = block
            put_cols(cbuf.at[0], dp, j, jnp.sum(block, axis=0, keepdims=True))
        return carry

    def low_part(q, carry):
        for i in range(2):
            cols = pl.ds(pl.multiple_of((2 * q + i) * W, W), W)
            unit = protos_v[q, :, W * i : W * i + W].astype(F32) * pinv[:, cols]
            plo[:, cols] = (unit - pc[:, cols].astype(F32)).astype(BF16)
        return carry

    lax.fori_loop(0, 4, front, 0)
    pl.semaphore_wait(barrier, 7 + len(FAR_FIRST))
    for q in range(4):
        send_cols(0, q)

    def send_rows(t):
        for dy, dz in FAR_FIRST:
            remote(rbuf.at[t, pr], rbuf.at[t, pr], r_ssem, r_rsem.at[t], proto_peer(dy, dz)).start()

    def take_rows(t):
        wait_bytes(rbuf.at[t, pl.ds(0, 31)], r_rsem.at[t])
        return jnp.sum(rbuf[t], axis=0)

    def spread(row):
        return jnp.transpose(jnp.broadcast_to(row, (128, 128)))

    def row_pass(t):
        for p in range(4):
            take_cols(t, p)
            for i in range(4):
                rows = slice(128 * i, 128 * i + 128)
                total = row_acc[rows, :] if p else jnp.zeros((128, 128), F32)
                for k in range(8 * p, 8 * p + 8):
                    total += expos[rows, 128 * k : 128 * k + 128] * vrow[k : k + 1, :]
                if p < 3:
                    row_acc[rows, :] = total
                else:
                    rbuf[t, pr, i : i + 1, :] = jnp.sum(
                        jnp.transpose(total), axis=0, keepdims=True
                    )

    def col_pass(t):
        def chunk(j, carry):
            cols = pl.ds(pl.multiple_of(j * 1024, 1024), 1024)
            sums = jnp.zeros((8, 1024), F32)
            for i in range(64):
                scale = ub[8 * i : 8 * i + 8, :]
                sums += expos[8 * i : 8 * i + 8, cols] * jnp.concatenate([scale] * 8, axis=1)
            total = jnp.sum(sums, axis=0, keepdims=True)
            for q in range(8):
                cbuf[t, dp, pl.ds(8 * j + q, 1), :] = total[:, 128 * q : 128 * q + 128]
            send_cols(t, j)
            return carry

        lax.fori_loop(0, 4, chunk, 0)

    def spread_rows(values, target):
        for i in range(4):
            target[128 * i : 128 * i + 128, :] = spread(values[i : i + 1, :])

    wait_bytes(student_v, in_sem.at[3])
    for i in range(4):
        unit, norm = masked(student_v, i)
        rows = slice(128 * i, 128 * i + 128)
        s_send[rows, :] = unit
        s_cast[rows, :] = unit.astype(BF16)
        s_inv[rows, :] = jnp.broadcast_to(1.0 / norm, (128, 128))
        s_unit_t[:, rows] = jnp.transpose(unit)
    ts = [
        remote(t_send, t_other, ts_ssem.at[0], ts_rsem.at[0], partner),
        remote(s_send, s_other, ts_ssem.at[1], ts_rsem.at[1], partner),
    ]
    for copy in ts:
        copy.start()

    half = core * 2048
    tot_acc[...] = jnp.zeros_like(tot_acc)
    fp[...] = jnp.zeros_like(fp)

    def student_cols(j, keep):
        at = lax.rem(j * W + half, 4096)
        cols = pl.ds(pl.multiple_of(at, W), W)
        block = jnp.exp2(dot(s_cast[...], pc[:, cols]) * student_scale)
        for q in range(W // 128):
            tot_acc[...] += block[:, 128 * q : 128 * q + 128]
        high, low = split(block)
        if keep:
            mine = pl.ds(pl.multiple_of(j * W, W), W)
            x2h[0:512, mine] = high
            x2l[0:512, mine] = low
        fp[...] += (
            dot_cols(high, pc[:, cols]) + dot_cols(low, pc[:, cols]) + dot_cols(high, plo[:, cols])
        )

    def student_mine(j, carry):
        student_cols(j, True)
        return carry

    def student_rest(j, carry):
        student_cols(j, False)
        return carry

    lax.fori_loop(0, 4, low_part, 0)
    lax.fori_loop(0, 2, student_mine, 0)
    row_pass(0)
    send_rows(0)

    lax.fori_loop(2, 4, student_mine, 0)
    lax.fori_loop(4, 8, student_rest, 0)
    for i in range(4):
        rbuf[3, pr, i : i + 1, :] = jnp.sum(
            jnp.transpose(tot_acc[128 * i : 128 * i + 128, :]), axis=0, keepdims=True
        )
    send_rows(3)
    spread_rows(1.0 / take_rows(0), ub)
    col_pass(1)

    def send_y(q, src, steps):
        for dy in steps:
            ty = lax.rem(y + dy, NY)
            remote(
                src.at[pl.ds(pl.multiple_of(ty * 128, 128), 128)], yr.at[q, dy - 1],
                y_ssem.at[q], y_rsem.at[q], proto_peer(dy, 0),
            ).start()

    def take_y(q, src):
        wait_bytes(yr.at[q], y_rsem.at[q])
        own = pl.ds(pl.multiple_of(y * 128, 128), 128)
        ysum[q] = src[own, :] + yr[q, 0] + yr[q, 1] + yr[q, 2]

    def send_z(q):
        for dz in (4, 3, 5, 2, 6, 1, 7):
            tz = lax.rem(z + dz, NZ)
            remote(
                ysum.at[q, pl.ds(pl.multiple_of(tz * 16, 16), 16)], zr.at[q, dz - 1],
                z_ssem, z_rsem.at[q], proto_peer(0, dz),
            ).start()

    def take_z(q):
        wait_bytes(zr.at[q], z_rsem.at[q])
        total = ysum[q, pl.ds(pl.multiple_of(z * 16, 16), 16), :]
        for k in range(7):
            total += zr[q, k]
        return total

    send_y(0, fp, (2,))
    for copy in ts:
        copy.wait_recv()
    t_cast[...] = t_other[...].astype(BF16)
    s_cast[...] = s_other[...].astype(BF16)

    def other_cols(j, carry):
        cols = pl.ds(pl.multiple_of(j * W + half, W), W)
        mine = pl.ds(pl.multiple_of(j * W, W), W)
        high, low = split(jnp.exp2(dot(t_cast[...], pc[:, cols]) * teacher_scale))
        e2h[512:1024, mine] = high
        e2l[512:1024, mine] = low
        high, low = split(jnp.exp2(dot(s_cast[...], pc[:, cols]) * student_scale))
        x2h[512:1024, mine] = high
        x2l[512:1024, mine] = low
        return carry

    lax.fori_loop(0, 4, other_cols, 0)
    for i in range(4):
        s_unit_t[:, 512 + 128 * i : 640 + 128 * i] = jnp.transpose(
            s_other[128 * i : 128 * i + 128, :]
        )
    row_pass(1)
    send_rows(1)

    def scale_half(at, ref):
        for i in range(4):
            cols = slice(at + 128 * i, at + 128 * i + 128)
            high, low = split(s_unit_t[:, cols] * ref[i : i + 1, :])
            a_hi[:, cols] = high
            a_lo[:, cols] = low

    tot_row[...] = 1.0 / take_rows(3)
    swap_s[0] = tot_row[...]
    swap_tot = remote(swap_s.at[0], swap_r.at[0], swap_ssem.at[0], swap_rsem.at[0], partner)
    swap_tot.start()
    spread_rows(tot_row[...], totb)
    def weigh_some(rows, cols, high, low):
        return (
            dot(a_hi[:, rows], high[rows, cols])
            + dot(a_lo[:, rows], high[rows, cols])
            + dot(a_hi[:, rows], low[rows, cols])
        )

    scale_half(0, tot_row)

    def probs_own(j, carry):
        mine = pl.ds(pl.multiple_of(j * W, W), W)
        wtp[:, mine] = weigh_some(slice(0, 512), mine, x2h, x2l)
        return carry

    lax.fori_loop(0, 4, probs_own, 0)
    swap_tot.wait_recv()
    scale_half(512, swap_r.at[0])

    def probs_other(j, carry):
        mine = pl.ds(pl.multiple_of(j * W, W), W)
        wtp[:, mine] += weigh_some(slice(512, 1024), mine, x2h, x2l)
        return carry

    lax.fori_loop(0, 4, probs_other, 0)
    spread_rows(1.0 / take_rows(1), ub)
    col_pass(2)

    send_y(0, fp, (1, 3))
    def own_split(j, carry):
        cols = pl.ds(pl.multiple_of(j * W + half, W), W)
        mine = pl.ds(pl.multiple_of(j * W, W), W)
        high, low = split(expos[:, cols])
        e2h[0:512, mine] = high
        e2l[0:512, mine] = low
        return carry

    lax.fori_loop(0, 4, own_split, 0)
    row_pass(2)
    send_rows(2)

    ft[...] = jnp.zeros_like(ft)

    def target_cols(q, carry):
        total = ft[...]
        for i in range(2):
            j = 2 * q + i
            cols = pl.ds(pl.multiple_of(j * W, W), W)
            inv = pinv[:, cols]
            scale = jnp.concatenate(
                [
                    inv[:, 128 * n : 128 * n + 128] * vrow[pl.ds(4 * j + n, 1), :]
                    for n in range(W // 128)
                ],
                axis=1,
            )
            b_high, b_low = split(protos_v[q, :, W * i : W * i + W].astype(F32) * scale)
            high, low = split(expos[:, cols])
            total += dot_cols(high, b_high) + dot_cols(low, b_high) + dot_cols(high, b_low)
        ft[...] = total
        return carry

    lax.fori_loop(0, 2, target_cols, 0)
    take_y(0, fp)
    send_z(0)
    lax.fori_loop(2, 4, target_cols, 0)
    for n, dz in enumerate(Z_FAR_FIRST):
        tz = lax.rem(z + dz, NZ) * 16
        for dy in (2, 1, 3):
            ty = lax.rem(y + dy, NY) * 128
            remote(
                ft.at[pl.ds(pl.multiple_of(ty + tz, 16), 16)], yr.at[1, dy - 1, pl.ds(pl.multiple_of(tz, 16), 16)],
                yp_ssem, yp_rsem.at[n // 4], proto_peer(dy, 0),
            ).start()
    swap_s[1] = 1.0 / take_rows(2)
    swap_u = remote(swap_s.at[1], swap_r.at[1], swap_ssem.at[1], swap_rsem.at[1], partner)
    swap_u.start()
    def block(d, offset, size):
        return pl.ds(pl.multiple_of(d * 64 + offset, 32), size)

    def protos_part(j, target):
        mine = pl.ds(pl.multiple_of(j * V, V), V)
        cols = pl.ds(pl.multiple_of(j * V + half, V), V)
        at = half // 128 + V // 128 * j
        target = jnp.concatenate(
            [
                target[:, 128 * q : 128 * q + 128] * vrow[pl.ds(at + q, 1), :]
                for q in range(V // 128)
            ],
            axis=1,
        )
        total = wtp[:, mine] - target
        inside = pl.ds(pl.multiple_of(lax.rem(j, 4) * V, V), V)
        unit = protos_v[2 * core + lax.div(j, 4), :, inside].astype(F32) * pinv[:, cols]
        inner = jnp.sum(unit * total, axis=0, keepdims=True)
        gpart[j] = (total - unit * inner) * (pinv[:, cols] * slope_scale)
        remote(gpart.at[j, block(x_far, 0, 32)], p1r.at[j, 0], p1_ssem, p1_rsem.at[j], right).start()
        remote(gpart.at[j, block(x_far, 32, 32)], p1r.at[j, 1], p1_ssem, p1_rsem.at[j], left).start()
        remote(gpart.at[j, block(x, 32 - 32 * core, 32)], p2r.at[j, 4], p2_ssem, p2_rsem.at[j], partner).start()

    first = pl.ds(0, V)
    scale_half(0, swap_s.at[1])
    target = weigh_some(slice(0, 512), first, e2h, e2l)
    swap_u.wait_recv()
    scale_half(512, swap_r.at[1])
    protos_part(0, target + weigh_some(slice(512, 1024), first, e2h, e2l))

    def protos_rest(j, carry):
        protos_part(j, weigh_some(slice(0, 1024), pl.ds(pl.multiple_of(j * V, V), V), e2h, e2l))
        return carry

    def take_pieces(first, last):
        wait_bytes(yr.at[1, pl.ds(0, 3), pl.ds(0, 64)], yp_rsem.at[first // 4])
        for dz in Z_FAR_FIRST[first:last]:
            tz = lax.rem(z + dz, NZ) * 16
            rows = pl.ds(pl.multiple_of(tz, 16), 16)
            own = pl.ds(pl.multiple_of(y * 128 + tz, 16), 16)
            ysum[1, rows, :] = ft[own, :] + yr[1, 0, rows, :] + yr[1, 1, rows, :] + yr[1, 2, rows, :]
            if dz:
                remote(
                    ysum.at[1, rows], zr.at[1, dz - 1], z_ssem, z_rsem.at[1], proto_peer(0, dz)
                ).start()

    def pass_on(j, carry):
        wait_bytes(p1r.at[j], p1_rsem.at[j])
        for s, side in enumerate((x_next, x_prev)):
            gpart[j, block(side, 32 * s, 32), :] += p1r[j, s]
            for c in range(2):
                remote(
                    gpart.at[j, block(side, 32 * c, 32)], p2r.at[j, 2 * s + core],
                    p2_ssem, p2_rsem.at[j], (side * 2 + c, pr),
                ).start()
        return carry

    lax.fori_loop(1, 5, protos_rest, 0)
    pass_on(0, 0)
    take_pieces(0, 4)
    lax.fori_loop(5, 8, protos_rest, 0)

    lax.fori_loop(1, 4, pass_on, 0)
    take_pieces(4, 8)
    lax.fori_loop(4, 6, pass_on, 0)
    spread_rows(swap_s[1], ub)

    own16 = pl.ds(pl.multiple_of(y * 128 + z * 16, 16), 16)
    by_probs = take_z(0)
    by_target = take_z(1)
    unit = s_send[own16, :]
    scale_p = jnp.concatenate([totb[own16, :]] * 2, axis=1)
    scale_t = jnp.concatenate([ub[own16, :]] * 2, axis=1)
    grad = slope_scale * (by_probs * scale_p - by_target * scale_t)
    inner = jnp.sum(unit * grad, axis=1, keepdims=True)
    ag[y, z] = (grad - unit * inner) * jnp.concatenate([s_inv[own16, :]] * 2, axis=1)
    for dz in (1, 7, 2, 6, 3, 5, 4):
        remote(ag.at[y, z], ag.at[y, z], agz_ssem, agz_rsem.at[dz - 1], proto_peer(0, dz)).start()

    def to_y(piece):
        for dy in (2, 1, 3):
            remote(piece, piece, agy_ssem, agy_rsem.at[dy - 1], proto_peer(dy, 0)).start()

    to_y(ag.at[y, z])
    lax.fori_loop(6, 8, pass_on, 0)

    def finish(j, carry):
        wait_bytes(p2r.at[j], p2_rsem.at[j])
        gw_ref[j, 0] = gpart[j, block(x, 32 * core, 32), :] + p2r[j, core] + p2r[j, 2 + core]
        gw_ref[j, 1] = p2r[j, 4] + p2r[j, 1 - core] + p2r[j, 3 - core]
        for i, start in enumerate((half, 2048 - half)):
            cols = pl.ds(pl.multiple_of(j * V + start, V), V)
            pltpu.make_async_copy(gw_ref.at[j, i], gw_hbm.at[:, cols], out_sem.at[0]).start()
        return carry

    for dz in (1, 7, 2, 6, 3, 5, 4):
        piece = ag.at[y, lax.rem(z + NZ - dz, NZ)]
        wait_bytes(piece, agz_rsem.at[dz - 1])
        to_y(piece)
    pltpu.make_async_copy(ag.at[y], rows_hbm.at[y], out_sem.at[1]).start()
    lax.fori_loop(0, 8, finish, 0)

    for dy in (1, 3, 2):
        image = lax.rem(y + NY - dy, NY)
        wait_bytes(ag.at[image], agy_rsem.at[dy - 1])
        pltpu.make_async_copy(ag.at[image], rows_hbm.at[image], out_sem.at[1]).start()

    wait_bytes(cbuf.at[:, pl.ds(0, 7)], c_ssem)
    wait_bytes(rbuf.at[:, pl.ds(0, 31)], r_ssem)
    for copy in ts:
        copy.wait_send()
    swap_tot.wait_send()
    swap_u.wait_send()
    wait_bytes(yr.at[0], y_ssem.at[0])
    wait_bytes(yr.at[1], yp_ssem)
    wait_bytes(zr, z_ssem)
    wait_bytes(ag.at[0, pl.ds(0, 7)], agz_ssem)
    wait_bytes(ag.at[pl.ds(0, 3)], agy_ssem)

    wait_bytes(p1r, p1_ssem)
    wait_bytes(p2r, p2_ssem)
    wait_bytes(gw_ref, out_sem.at[0])
    wait_bytes(ag, out_sem.at[1])


def place_kernel(rows_hbm, index_hbm, gw_in, gp_hbm, gw_hbm, rows, index, placed, gw, sem, out_sem):
    gw_load = pltpu.make_async_copy(gw_in, gw, sem.at[5])
    loads = [pltpu.make_async_copy(rows_hbm.at[i], rows.at[i], sem.at[i]) for i in range(4)]
    index_load = pltpu.make_async_copy(index_hbm, index, sem.at[4])
    for copy in [*loads, index_load, gw_load]:
        copy.start()
    index_load.wait()
    onehots = []
    for i in range(4):
        places = lax.broadcasted_iota(jnp.int32, (256, 128), 0)
        onehots.append(jnp.where(places == index[i : i + 1, :], 1.0, 0.0).astype(BF16))
    for copy in loads:
        copy.wait()
    stores = []
    for i in range(4):
        high, low = split(rows[i])
        placed[i] = dot(onehots[i], high) + dot(onehots[i], low)
        stores.append(
            pltpu.make_async_copy(placed.at[i], gp_hbm.at[pl.ds(256 * i, 256)], out_sem.at[i])
        )
        stores[-1].start()
        if i == 1:
            gw_load.wait()
            stores.append(pltpu.make_async_copy(gw, gw_hbm, out_sem.at[4]))
            stores[-1].start()
    for copy in stores:
        copy.wait()


def body(student_patches, teacher_patches, masked_index, prototypes):
    dma = pltpu.SemaphoreType.DMA

    def vmem(*shape, dtype=F32):
        return pltpu.VMEM(shape, dtype)

    def half_vmem(*shape):
        return pltpu.VMEM(shape, BF16)

    scratch = [
        half_vmem(1024, 256), half_vmem(1024, 256), vmem(4, 128, dtype=jnp.int32), half_vmem(4, 256, 1024), dma((4,)), dma((4,)),
        half_vmem(4, 256, 128), vmem(512, 256), vmem(512, 256), vmem(512, 256), vmem(512, 256),
        half_vmem(512, 256), half_vmem(512, 256), vmem(256, 1024), vmem(512, 128),
        half_vmem(256, 4096), half_vmem(256, 4096), vmem(1, 4096), vmem(512, 4096),
        half_vmem(1024, 2048), half_vmem(1024, 2048), half_vmem(1024, 2048), half_vmem(1024, 2048),
        vmem(256, 2048), half_vmem(256, 1024), half_vmem(256, 1024),
        vmem(3, 8, 32, 128), dma, dma((3, 4)),
        vmem(4, 32, 4, 128), dma, dma((4,)),
        vmem(512, 128), vmem(512, 128), vmem(32, 128), vmem(4, 128), vmem(512, 128), vmem(512, 128),
        dma((2,)), dma((2,)), vmem(2, 4, 128), vmem(2, 4, 128), dma((2,)), dma((2,)),
        vmem(512, 256), vmem(512, 256), vmem(2, 3, 128, 256), vmem(2, 128, 256), dma((1,)), dma((1,)), dma, dma((2,)),
        vmem(2, 7, 16, 256), dma, dma((2,)),
        vmem(4, 8, 16, 256), dma, dma((7,)), dma, dma((3,)),
        vmem(8, 256, 256), vmem(8, 2, 32, 256), dma, dma((8,)),
        vmem(8, 5, 32, 256), dma, dma((8,)), vmem(8, 2, 32, 256), dma((2,)),
    ]
    anywhere = pl.BlockSpec(memory_space=pl.ANY)
    rows, grad_prototypes = pl.pallas_call(
        kernel,
        out_shape=(
            jax.ShapeDtypeStruct((4, 8, 16, 256), F32),
            jax.ShapeDtypeStruct((32, 4096), F32),
        ),
        in_specs=[anywhere] * 4,
        out_specs=(anywhere, anywhere),
        scratch_shapes=scratch,
        compiler_params=pltpu.CompilerParams(
            collective_id=0, has_side_effects=True, vmem_limit_bytes=60 * 1024 * 1024
        ),
    )(student_patches, teacher_patches, masked_index, prototypes)
    return pl.pallas_call(
        place_kernel,
        out_shape=(
            jax.ShapeDtypeStruct((1024, 256), F32),
            jax.ShapeDtypeStruct((32, 4096), F32),
        ),
        in_specs=[anywhere] * 3,
        out_specs=(anywhere, anywhere),
        scratch_shapes=[
            vmem(4, 128, 256), vmem(4, 128, dtype=jnp.int32), vmem(4, 256, 256), vmem(32, 4096), dma((6,)), dma((5,)),
        ],
    )(rows.reshape(4, 128, 256), masked_index, grad_prototypes)


def solution(mesh):
    placed = (P("dp", None), P("dp", None), P("dp", None), P(None, "proto"))
    return jax.shard_map(
        body,
        mesh=mesh,
        in_specs=placed,
        out_specs=(P("dp", None), P("dp", "proto")),
        check_vma=False,
    )
```

```python
import math

import jax
import jax.numpy as jnp
from jax import lax
from jax.experimental import pallas as pl
from jax.experimental.pallas import tpu as pltpu
from jax.sharding import PartitionSpec as P

MESH = pl.DeviceIdType.MESH
F32 = jnp.float32
BF16 = jnp.bfloat16

teacher_scale = math.log2(math.e) / 0.07
student_scale = math.log2(math.e) / 0.1
slope_scale = 4096.0 / 0.1
epsilon = 1e-06

W = 512
V = 256
NY, NZ = 4, 8
Z_FAR_FIRST = (4, 3, 5, 2, 6, 1, 7, 0)
FAR_FIRST = sorted(
    [(dy, dz) for dy in range(NY) for dz in range(NZ) if dy or dz],
    key=lambda o: -(min(o[0], NY - o[0]) + min(o[1], NZ - o[1])),
)


def dot(a, b):
    return jnp.dot(a, b, preferred_element_type=F32)


def dot_cols(a, b):
    return lax.dot_general(a, b, (((1,), (1,)), ((), ())), preferred_element_type=F32)


def split(value):
    high = value.astype(BF16)
    return high, (value - high.astype(F32)).astype(BF16)


def kernel(
    student_hbm, teacher_hbm, index_hbm, protos_hbm,
    rows_hbm, gw_hbm,
    student_v, teacher_v, index_v, protos_v, in_sem, protos_sem,
    onehot, t_send, s_send, t_other, s_other, t_cast, s_cast, s_unit_t, s_inv,
    pc, plo, pinv, expos,
    e2h, e2l, x2h, x2l, wtp, a_hi, a_lo,
    cbuf, c_ssem, c_rsem,
    rbuf, r_ssem, r_rsem, ub, row_acc, vrow, tot_row, tot_acc, totb,
    ts_ssem, ts_rsem, swap_s, swap_r, swap_ssem, swap_rsem,
    fp, ft, yr, ysum, y_ssem, y_rsem, yp_ssem, yp_rsem, zr, z_ssem, z_rsem,
    ag, agz_ssem, agz_rsem, agy_ssem, agy_rsem,
    gpart, p1r, p1_ssem, p1_rsem, p2r, p2_ssem, p2_rsem,
    gw_ref, out_sem,
):
    dp = lax.axis_index("dp")
    pr = lax.axis_index("proto")
    x, core = lax.div(dp, 2), lax.rem(dp, 2)
    y, z = lax.div(pr, NZ), lax.rem(pr, NZ)
    x_next, x_prev, x_far = lax.rem(x + 1, 4), lax.rem(x + 3, 4), lax.rem(x + 2, 4)
    right = (x_next * 2 + core, pr)
    left = (x_prev * 2 + core, pr)
    partner = (x * 2 + 1 - core, pr)

    def dp_peer(k):
        return (lax.rem(dp + k, 8), pr)

    def proto_peer(dy, dz):
        return (dp, lax.rem(y + dy, NY) * NZ + lax.rem(z + dz, NZ))

    def remote(src, dst, ssem, rsem, device):
        return pltpu.make_async_remote_copy(
            src, dst, ssem, rsem, device_id=device, device_id_type=MESH
        )

    def wait_bytes(ref, sem):
        pltpu.make_async_copy(ref, ref, sem).wait()

    def load(src, dst, sem, parts):
        size = src.shape[0] // parts
        for i in range(parts):
            rows = pl.ds(i * size, size)
            pltpu.make_async_copy(src.at[rows], dst.at[rows], sem).start()

    load(index_hbm, index_v, in_sem.at[0], 1)
    load(teacher_hbm, teacher_v, in_sem.at[1], 4)
    barrier = pltpu.get_barrier_semaphore()
    for k in range(1, 8):
        pl.semaphore_signal(barrier, inc=1, device_id=dp_peer(k), device_id_type=MESH)
    for dy, dz in FAR_FIRST:
        pl.semaphore_signal(
            barrier, inc=1, device_id=proto_peer(dy, dz), device_id_type=MESH
        )
    for j in range(4):
        cols = pl.ds(2 * W * j, 2 * W)
        pltpu.make_async_copy(protos_hbm.at[:, cols], protos_v.at[j], protos_sem.at[j]).start()
    load(student_hbm, student_v, in_sem.at[3], 4)

    wait_bytes(index_v, in_sem.at[0])
    for i in range(4):
        places = lax.broadcasted_iota(jnp.int32, (256, 128), 0)
        onehot[i] = jnp.where(places == index_v[i : i + 1, :], 1.0, 0.0).astype(BF16)

    def masked(patches, i):
        rows = lax.dot_general(
            onehot[i], patches[256 * i : 256 * i + 256, :],
            (((0,), (0,)), ((), ())), preferred_element_type=F32,
        )
        norm = jnp.sqrt(jnp.sum(rows * rows, axis=1, keepdims=True) + epsilon)
        return rows / norm, norm

    wait_bytes(teacher_v, in_sem.at[1])
    for i in range(4):
        unit, _ = masked(teacher_v, i)
        t_send[128 * i : 128 * i + 128, :] = unit
        t_cast[128 * i : 128 * i + 128, :] = unit.astype(BF16)

    def put_cols(buf, slot, j, sums):
        for q in range(W // 128):
            buf[slot, pl.ds(4 * j + q, 1), :] = sums[:, 128 * q : 128 * q + 128]


    def send_cols(t, q):
        piece = cbuf.at[t, dp, pl.ds(pl.multiple_of(8 * q, 8), 8)]
        for k in (4, 3, 5, 2, 6, 1, 7):
            remote(piece, piece, c_ssem, c_rsem.at[t, q], dp_peer(k)).start()

    def take_cols(t, q):
        rows = slice(8 * q, 8 * q + 8)
        wait_bytes(cbuf.at[t, pl.ds(0, 7), rows], c_rsem.at[t, q])
        vrow[rows, :] = 1.0 / jnp.sum(cbuf[t, :, rows, :], axis=0)

    def front(p, carry):
        for i in range(2):
            wait_bytes(protos_v.at[2 * p + i], protos_sem.at[2 * p + i])
        for i in range(4):
            j = 4 * p + i
            cols = pl.ds(pl.multiple_of(j * W, W), W)
            weights = protos_v[2 * p + i // 2, :, W * (i % 2) : W * (i % 2) + W].astype(F32)
            inv = 1.0 / jnp.sqrt(jnp.sum(weights * weights, axis=0, keepdims=True) + epsilon)
            pinv[:, cols] = inv
            unit = (weights * inv).astype(BF16)
            pc[:, cols] = unit
            block = jnp.exp2(dot(t_cast[...], unit) * teacher_scale)
            expos[:, cols] = block
            put_cols(cbuf.at[0], dp, j, jnp.sum(block, axis=0, keepdims=True))
        return carry

    def low_part(q, carry):
        for i in range(2):
            cols = pl.ds(pl.multiple_of((2 * q + i) * W, W), W)
            unit = protos_v[q, :, W * i : W * i + W].astype(F32) * pinv[:, cols]
            plo[:, cols] = (unit - pc[:, cols].astype(F32)).astype(BF16)
        return carry

    lax.fori_loop(0, 2, front, 0)
    pl.semaphore_wait(barrier, 7 + len(FAR_FIRST))
    for q in range(4):
        send_cols(0, q)

    def send_rows(t):
        for dy, dz in FAR_FIRST:
            remote(rbuf.at[t, pr], rbuf.at[t, pr], r_ssem, r_rsem.at[t], proto_peer(dy, dz)).start()

    def take_rows(t):
        wait_bytes(rbuf.at[t, pl.ds(0, 31)], r_rsem.at[t])
        return jnp.sum(rbuf[t], axis=0)

    def spread(row):
        return jnp.transpose(jnp.broadcast_to(row, (128, 128)))

    def row_pass(t):
        for p in range(4):
            take_cols(t, p)
            for i in range(4):
                rows = slice(128 * i, 128 * i + 128)
                total = row_acc[rows, :] if p else jnp.zeros((128, 128), F32)
                for k in range(8 * p, 8 * p + 8):
                    total += expos[rows, 128 * k : 128 * k + 128] * vrow[k : k + 1, :]
                if p < 3:
                    row_acc[rows, :] = total
                else:
                    rbuf[t, pr, i : i + 1, :] = jnp.sum(
                        jnp.transpose(total), axis=0, keepdims=True
                    )

    def col_pass(t):
        def chunk(j, carry):
            cols = pl.ds(pl.multiple_of(j * 1024, 1024), 1024)
            sums = jnp.zeros((8, 1024), F32)
            for i in range(64):
                scale = ub[8 * i : 8 * i + 8, :]
                sums += expos[8 * i : 8 * i + 8, cols] * jnp.concatenate([scale] * 8, axis=1)
            total = jnp.sum(sums, axis=0, keepdims=True)
            for q in range(8):
                cbuf[t, dp, pl.ds(8 * j + q, 1), :] = total[:, 128 * q : 128 * q + 128]
            send_cols(t, j)
            return carry

        lax.fori_loop(0, 4, chunk, 0)

    def spread_rows(values, target):
        for i in range(4):
            target[128 * i : 128 * i + 128, :] = spread(values[i : i + 1, :])

    wait_bytes(student_v, in_sem.at[3])
    for i in range(4):
        unit, norm = masked(student_v, i)
        rows = slice(128 * i, 128 * i + 128)
        s_send[rows, :] = unit
        s_cast[rows, :] = unit.astype(BF16)
        s_inv[rows, :] = jnp.broadcast_to(1.0 / norm, (128, 128))
        s_unit_t[:, rows] = jnp.transpose(unit)
    ts = [
        remote(t_send, t_other, ts_ssem.at[0], ts_rsem.at[0], partner),
        remote(s_send, s_other, ts_ssem.at[1], ts_rsem.at[1], partner),
    ]
    for copy in ts:
        copy.start()

    half = core * 2048
    tot_acc[...] = jnp.zeros_like(tot_acc)
    fp[...] = jnp.zeros_like(fp)

    def student_cols(j, keep):
        at = lax.rem(j * W + half, 4096)
        cols = pl.ds(pl.multiple_of(at, W), W)
        block = jnp.exp2(dot(s_cast[...], pc[:, cols]) * student_scale)
        for q in range(W // 128):
            tot_acc[...] += block[:, 128 * q : 128 * q + 128]
        high, low = split(block)
        if keep:
            mine = pl.ds(pl.multiple_of(j * W, W), W)
            x2h[0:512, mine] = high
            x2l[0:512, mine] = low
        fp[...] += (
            dot_cols(high, pc[:, cols]) + dot_cols(low, pc[:, cols]) + dot_cols(high, plo[:, cols])
        )

    def student_mine(j, carry):
        student_cols(j, True)
        return carry

    def student_rest(j, carry):
        student_cols(j, False)
        return carry

    lax.fori_loop(0, 4, low_part, 0)
    lax.fori_loop(0, 2, student_mine, 0)
    row_pass(0)
    send_rows(0)

    lax.fori_loop(2, 4, student_mine, 0)
    lax.fori_loop(4, 8, student_rest, 0)
    for i in range(4):
        rbuf[3, pr, i : i + 1, :] = jnp.sum(
            jnp.transpose(tot_acc[128 * i : 128 * i + 128, :]), axis=0, keepdims=True
        )
    send_rows(3)
    spread_rows(1.0 / take_rows(0), ub)
    col_pass(1)

    def send_y(q, src, steps):
        for dy in steps:
            ty = lax.rem(y + dy, NY)
            remote(
                src.at[pl.ds(pl.multiple_of(ty * 128, 128), 128)], yr.at[q, dy - 1],
                y_ssem.at[q], y_rsem.at[q], proto_peer(dy, 0),
            ).start()

    def take_y(q, src):
        wait_bytes(yr.at[q], y_rsem.at[q])
        own = pl.ds(pl.multiple_of(y * 128, 128), 128)
        ysum[q] = src[own, :] + yr[q, 0] + yr[q, 1] + yr[q, 2]

    def send_z(q):
        for dz in (4, 3, 5, 2, 6, 1, 7):
            tz = lax.rem(z + dz, NZ)
            remote(
                ysum.at[q, pl.ds(pl.multiple_of(tz * 16, 16), 16)], zr.at[q, dz - 1],
                z_ssem, z_rsem.at[q], proto_peer(0, dz),
            ).start()

    def take_z(q):
        wait_bytes(zr.at[q], z_rsem.at[q])
        total = ysum[q, pl.ds(pl.multiple_of(z * 16, 16), 16), :]
        for k in range(7):
            total += zr[q, k]
        return total

    send_y(0, fp, (2,))
    for copy in ts:
        copy.wait_recv()
    t_cast[...] = t_other[...].astype(BF16)
    s_cast[...] = s_other[...].astype(BF16)

    def other_cols(j, carry):
        cols = pl.ds(pl.multiple_of(j * W + half, W), W)
        mine = pl.ds(pl.multiple_of(j * W, W), W)
        high, low = split(jnp.exp2(dot(t_cast[...], pc[:, cols]) * teacher_scale))
        e2h[512:1024, mine] = high
        e2l[512:1024, mine] = low
        high, low = split(jnp.exp2(dot(s_cast[...], pc[:, cols]) * student_scale))
        x2h[512:1024, mine] = high
        x2l[512:1024, mine] = low
        return carry

    lax.fori_loop(0, 4, other_cols, 0)
    for i in range(4):
        s_unit_t[:, 512 + 128 * i : 640 + 128 * i] = jnp.transpose(
            s_other[128 * i : 128 * i + 128, :]
        )
    row_pass(1)
    send_rows(1)

    def scale_half(at, ref):
        for i in range(4):
            cols = slice(at + 128 * i, at + 128 * i + 128)
            high, low = split(s_unit_t[:, cols] * ref[i : i + 1, :])
            a_hi[:, cols] = high
            a_lo[:, cols] = low

    tot_row[...] = 1.0 / take_rows(3)
    swap_s[0] = tot_row[...]
    swap_tot = remote(swap_s.at[0], swap_r.at[0], swap_ssem.at[0], swap_rsem.at[0], partner)
    swap_tot.start()
    spread_rows(tot_row[...], totb)
    def weigh_some(rows, cols, high, low):
        return (
            dot(a_hi[:, rows], high[rows, cols])
            + dot(a_lo[:, rows], high[rows, cols])
            + dot(a_hi[:, rows], low[rows, cols])
        )

    scale_half(0, tot_row)

    def probs_own(j, carry):
        mine = pl.ds(pl.multiple_of(j * W, W), W)
        wtp[:, mine] = weigh_some(slice(0, 512), mine, x2h, x2l)
        return carry

    lax.fori_loop(0, 4, probs_own, 0)
    swap_tot.wait_recv()
    scale_half(512, swap_r.at[0])

    def probs_other(j, carry):
        mine = pl.ds(pl.multiple_of(j * W, W), W)
        wtp[:, mine] += weigh_some(slice(512, 1024), mine, x2h, x2l)
        return carry

    lax.fori_loop(0, 4, probs_other, 0)
    spread_rows(1.0 / take_rows(1), ub)
    col_pass(2)

    send_y(0, fp, (1, 3))
    def own_split(j, carry):
        cols = pl.ds(pl.multiple_of(j * W + half, W), W)
        mine = pl.ds(pl.multiple_of(j * W, W), W)
        high, low = split(expos[:, cols])
        e2h[0:512, mine] = high
        e2l[0:512, mine] = low
        return carry

    lax.fori_loop(0, 4, own_split, 0)
    row_pass(2)
    send_rows(2)

    ft[...] = jnp.zeros_like(ft)

    def target_cols(q, carry):
        total = ft[...]
        for i in range(2):
            j = 2 * q + i
            cols = pl.ds(pl.multiple_of(j * W, W), W)
            inv = pinv[:, cols]
            scale = jnp.concatenate(
                [
                    inv[:, 128 * n : 128 * n + 128] * vrow[pl.ds(4 * j + n, 1), :]
                    for n in range(W // 128)
                ],
                axis=1,
            )
            b_high, b_low = split(protos_v[q, :, W * i : W * i + W].astype(F32) * scale)
            high, low = split(expos[:, cols])
            total += dot_cols(high, b_high) + dot_cols(low, b_high) + dot_cols(high, b_low)
        ft[...] = total
        return carry

    lax.fori_loop(0, 2, target_cols, 0)
    take_y(0, fp)
    send_z(0)
    lax.fori_loop(2, 4, target_cols, 0)
    for n, dz in enumerate(Z_FAR_FIRST):
        tz = lax.rem(z + dz, NZ) * 16
        for dy in (2, 1, 3):
            ty = lax.rem(y + dy, NY) * 128
            remote(
                ft.at[pl.ds(pl.multiple_of(ty + tz, 16), 16)], yr.at[1, dy - 1, pl.ds(pl.multiple_of(tz, 16), 16)],
                yp_ssem, yp_rsem.at[n // 4], proto_peer(dy, 0),
            ).start()
    swap_s[1] = 1.0 / take_rows(2)
    swap_u = remote(swap_s.at[1], swap_r.at[1], swap_ssem.at[1], swap_rsem.at[1], partner)
    swap_u.start()
    def block(d, offset, size):
        return pl.ds(pl.multiple_of(d * 64 + offset, 32), size)

    def protos_part(j, target):
        mine = pl.ds(pl.multiple_of(j * V, V), V)
        cols = pl.ds(pl.multiple_of(j * V + half, V), V)
        at = half // 128 + V // 128 * j
        target = jnp.concatenate(
            [
                target[:, 128 * q : 128 * q + 128] * vrow[pl.ds(at + q, 1), :]
                for q in range(V // 128)
            ],
            axis=1,
        )
        total = wtp[:, mine] - target
        inside = pl.ds(pl.multiple_of(lax.rem(j, 4) * V, V), V)
        unit = protos_v[2 * core + lax.div(j, 4), :, inside].astype(F32) * pinv[:, cols]
        inner = jnp.sum(unit * total, axis=0, keepdims=True)
        gpart[j] = (total - unit * inner) * (pinv[:, cols] * slope_scale)
        remote(gpart.at[j, block(x_far, 0, 32)], p1r.at[j, 0], p1_ssem, p1_rsem.at[j], right).start()
        remote(gpart.at[j, block(x_far, 32, 32)], p1r.at[j, 1], p1_ssem, p1_rsem.at[j], left).start()
        remote(gpart.at[j, block(x, 32 - 32 * core, 32)], p2r.at[j, 4], p2_ssem, p2_rsem.at[j], partner).start()

    first = pl.ds(0, V)
    scale_half(0, swap_s.at[1])
    target = weigh_some(slice(0, 512), first, e2h, e2l)
    swap_u.wait_recv()
    scale_half(512, swap_r.at[1])
    protos_part(0, target + weigh_some(slice(512, 1024), first, e2h, e2l))

    def protos_rest(j, carry):
        protos_part(j, weigh_some(slice(0, 1024), pl.ds(pl.multiple_of(j * V, V), V), e2h, e2l))
        return carry

    def take_pieces(first, last):
        wait_bytes(yr.at[1, pl.ds(0, 3), pl.ds(0, 64)], yp_rsem.at[first // 4])
        for dz in Z_FAR_FIRST[first:last]:
            tz = lax.rem(z + dz, NZ) * 16
            rows = pl.ds(pl.multiple_of(tz, 16), 16)
            own = pl.ds(pl.multiple_of(y * 128 + tz, 16), 16)
            ysum[1, rows, :] = ft[own, :] + yr[1, 0, rows, :] + yr[1, 1, rows, :] + yr[1, 2, rows, :]
            if dz:
                remote(
                    ysum.at[1, rows], zr.at[1, dz - 1], z_ssem, z_rsem.at[1], proto_peer(0, dz)
                ).start()

    def pass_on(j, carry):
        wait_bytes(p1r.at[j], p1_rsem.at[j])
        for s, side in enumerate((x_next, x_prev)):
            gpart[j, block(side, 32 * s, 32), :] += p1r[j, s]
            for c in range(2):
                remote(
                    gpart.at[j, block(side, 32 * c, 32)], p2r.at[j, 2 * s + core],
                    p2_ssem, p2_rsem.at[j], (side * 2 + c, pr),
                ).start()
        return carry

    lax.fori_loop(1, 5, protos_rest, 0)
    pass_on(0, 0)
    take_pieces(0, 4)
    lax.fori_loop(5, 8, protos_rest, 0)

    lax.fori_loop(1, 4, pass_on, 0)
    take_pieces(4, 8)
    lax.fori_loop(4, 6, pass_on, 0)
    spread_rows(swap_s[1], ub)

    own16 = pl.ds(pl.multiple_of(y * 128 + z * 16, 16), 16)
    by_probs = take_z(0)
    by_target = take_z(1)
    unit = s_send[own16, :]
    scale_p = jnp.concatenate([totb[own16, :]] * 2, axis=1)
    scale_t = jnp.concatenate([ub[own16, :]] * 2, axis=1)
    grad = slope_scale * (by_probs * scale_p - by_target * scale_t)
    inner = jnp.sum(unit * grad, axis=1, keepdims=True)
    ag[y, z] = (grad - unit * inner) * jnp.concatenate([s_inv[own16, :]] * 2, axis=1)
    for dz in (1, 7, 2, 6, 3, 5, 4):
        remote(ag.at[y, z], ag.at[y, z], agz_ssem, agz_rsem.at[dz - 1], proto_peer(0, dz)).start()

    def to_y(piece):
        for dy in (2, 1, 3):
            remote(piece, piece, agy_ssem, agy_rsem.at[dy - 1], proto_peer(dy, 0)).start()

    to_y(ag.at[y, z])
    lax.fori_loop(6, 8, pass_on, 0)

    def finish(j, carry):
        wait_bytes(p2r.at[j], p2_rsem.at[j])
        gw_ref[j, 0] = gpart[j, block(x, 32 * core, 32), :] + p2r[j, core] + p2r[j, 2 + core]
        gw_ref[j, 1] = p2r[j, 4] + p2r[j, 1 - core] + p2r[j, 3 - core]
        for i, start in enumerate((half, 2048 - half)):
            cols = pl.ds(pl.multiple_of(j * V + start, V), V)
            pltpu.make_async_copy(gw_ref.at[j, i], gw_hbm.at[:, cols], out_sem.at[0]).start()
        return carry

    for dz in (1, 7, 2, 6, 3, 5, 4):
        piece = ag.at[y, lax.rem(z + NZ - dz, NZ)]
        wait_bytes(piece, agz_rsem.at[dz - 1])
        to_y(piece)
    pltpu.make_async_copy(ag.at[y], rows_hbm.at[y], out_sem.at[1]).start()
    lax.fori_loop(0, 8, finish, 0)

    for dy in (1, 3, 2):
        image = lax.rem(y + NY - dy, NY)
        wait_bytes(ag.at[image], agy_rsem.at[dy - 1])
        pltpu.make_async_copy(ag.at[image], rows_hbm.at[image], out_sem.at[1]).start()

    wait_bytes(cbuf.at[:, pl.ds(0, 7)], c_ssem)
    wait_bytes(rbuf.at[:, pl.ds(0, 31)], r_ssem)
    for copy in ts:
        copy.wait_send()
    swap_tot.wait_send()
    swap_u.wait_send()
    wait_bytes(yr.at[0], y_ssem.at[0])
    wait_bytes(yr.at[1], yp_ssem)
    wait_bytes(zr, z_ssem)
    wait_bytes(ag.at[0, pl.ds(0, 7)], agz_ssem)
    wait_bytes(ag.at[pl.ds(0, 3)], agy_ssem)

    wait_bytes(p1r, p1_ssem)
    wait_bytes(p2r, p2_ssem)
    wait_bytes(gw_ref, out_sem.at[0])
    wait_bytes(ag, out_sem.at[1])


def place_kernel(rows, index, gw, gp_hbm, gw_hbm, placed, out_sem):
    stores = [pltpu.make_async_copy(gw, gw_hbm, out_sem.at[4])]
    stores[0].start()
    for i in range(4):
        places = lax.broadcasted_iota(jnp.int32, (256, 128), 0)
        onehot = jnp.where(places == index[i : i + 1, :], 1.0, 0.0).astype(BF16)
        high, low = split(rows[i].reshape(128, 256))
        placed[i] = dot(onehot, high) + dot(onehot, low)
        stores.append(
            pltpu.make_async_copy(placed.at[i], gp_hbm.at[pl.ds(256 * i, 256)], out_sem.at[i])
        )
        stores[-1].start()
    for copy in stores:
        copy.wait()


def body(student_patches, teacher_patches, masked_index, prototypes):
    dma = pltpu.SemaphoreType.DMA

    def vmem(*shape, dtype=F32):
        return pltpu.VMEM(shape, dtype)

    def half_vmem(*shape):
        return pltpu.VMEM(shape, BF16)

    scratch = [
        half_vmem(1024, 256), half_vmem(1024, 256), vmem(4, 128, dtype=jnp.int32), half_vmem(4, 256, 1024), dma((4,)), dma((4,)),
        half_vmem(4, 256, 128), vmem(512, 256), vmem(512, 256), vmem(512, 256), vmem(512, 256),
        half_vmem(512, 256), half_vmem(512, 256), vmem(256, 1024), vmem(512, 128),
        half_vmem(256, 4096), half_vmem(256, 4096), vmem(1, 4096), vmem(512, 4096),
        half_vmem(1024, 2048), half_vmem(1024, 2048), half_vmem(1024, 2048), half_vmem(1024, 2048),
        vmem(256, 2048), half_vmem(256, 1024), half_vmem(256, 1024),
        vmem(3, 8, 32, 128), dma, dma((3, 4)),
        vmem(4, 32, 4, 128), dma, dma((4,)),
        vmem(512, 128), vmem(512, 128), vmem(32, 128), vmem(4, 128), vmem(512, 128), vmem(512, 128),
        dma((2,)), dma((2,)), vmem(2, 4, 128), vmem(2, 4, 128), dma((2,)), dma((2,)),
        vmem(512, 256), vmem(512, 256), vmem(2, 3, 128, 256), vmem(2, 128, 256), dma((1,)), dma((1,)), dma, dma((2,)),
        vmem(2, 7, 16, 256), dma, dma((2,)),
        vmem(4, 8, 16, 256), dma, dma((7,)), dma, dma((3,)),
        vmem(8, 256, 256), vmem(8, 2, 32, 256), dma, dma((8,)),
        vmem(8, 5, 32, 256), dma, dma((8,)), vmem(8, 2, 32, 256), dma((2,)),
    ]
    anywhere = pl.BlockSpec(memory_space=pl.ANY)
    rows, grad_prototypes = pl.pallas_call(
        kernel,
        out_shape=(
            pltpu.VMEM((4, 8, 16, 256), F32),
            pltpu.VMEM((32, 4096), F32),
        ),
        in_specs=[anywhere] * 4,
        out_specs=(anywhere, anywhere),
        scratch_shapes=scratch,
        compiler_params=pltpu.CompilerParams(
            collective_id=0, has_side_effects=True, vmem_limit_bytes=60 * 1024 * 1024
        ),
    )(student_patches, teacher_patches, masked_index, prototypes)
    return pl.pallas_call(
        place_kernel,
        out_shape=(
            jax.ShapeDtypeStruct((1024, 256), F32),
            jax.ShapeDtypeStruct((32, 4096), F32),
        ),
        in_specs=[pl.BlockSpec(memory_space=pltpu.VMEM)] * 3,
        out_specs=(anywhere, anywhere),
        scratch_shapes=[vmem(4, 256, 256), dma((5,))],
    )(
        pltpu.with_memory_space_constraint(rows, pltpu.VMEM),
        masked_index,
        pltpu.with_memory_space_constraint(grad_prototypes, pltpu.VMEM),
    )


def solution(mesh):
    placed = (P("dp", None), P("dp", None), P("dp", None), P(None, "proto"))
    return jax.shard_map(
        body,
        mesh=mesh,
        in_specs=placed,
        out_specs=(P("dp", None), P("dp", "proto")),
        check_vma=False,
    )
```

```python
import math

import jax
import jax.numpy as jnp
from jax import lax
from jax.experimental import pallas as pl
from jax.experimental.pallas import tpu as pltpu
from jax.sharding import PartitionSpec as P

MESH = pl.DeviceIdType.MESH
F32 = jnp.float32
BF16 = jnp.bfloat16

teacher_scale = math.log2(math.e) / 0.07
student_scale = math.log2(math.e) / 0.1
slope_scale = 4096.0 / 0.1
epsilon = 1e-06

W = 512
V = 256
NY, NZ = 4, 8
Z_FAR_FIRST = (4, 3, 5, 2, 6, 1, 7, 0)
FAR_FIRST = sorted(
    [(dy, dz) for dy in range(NY) for dz in range(NZ) if dy or dz],
    key=lambda o: -(min(o[0], NY - o[0]) + min(o[1], NZ - o[1])),
)


def dot(a, b):
    return jnp.dot(a, b, preferred_element_type=F32)


def dot_cols(a, b):
    return lax.dot_general(a, b, (((1,), (1,)), ((), ())), preferred_element_type=F32)


def split(value):
    high = value.astype(BF16)
    return high, (value - high.astype(F32)).astype(BF16)


def kernel(
    student_hbm, teacher_hbm, index_hbm, protos_hbm,
    rows_hbm, gw_hbm,
    student_v, teacher_v, index_v, protos_v, in_sem, protos_sem,
    onehot, t_send, s_send, t_other, s_other, t_cast, s_cast, s_unit_t, s_inv,
    pc, plo, pinv, expos,
    e2h, e2l, x2h, x2l, wtp, a_hi, a_lo,
    cbuf, c_ssem, c_rsem,
    rbuf, r_ssem, r_rsem, ub, row_acc, vrow, tot_row, tot_acc, totb,
    ts_ssem, ts_rsem, swap_s, swap_r, swap_ssem, swap_rsem,
    fp, ft, yr, ysum, y_ssem, y_rsem, yp_ssem, yp_rsem, zr, z_ssem, z_rsem,
    ag, agz_ssem, agz_rsem, agy_ssem, agy_rsem,
    gpart, p1r, p1_ssem, p1_rsem, p2r, p2_ssem, p2_rsem,
):
    dp = lax.axis_index("dp")
    pr = lax.axis_index("proto")
    x, core = lax.div(dp, 2), lax.rem(dp, 2)
    y, z = lax.div(pr, NZ), lax.rem(pr, NZ)
    x_next, x_prev, x_far = lax.rem(x + 1, 4), lax.rem(x + 3, 4), lax.rem(x + 2, 4)
    right = (x_next * 2 + core, pr)
    left = (x_prev * 2 + core, pr)
    partner = (x * 2 + 1 - core, pr)

    def dp_peer(k):
        return (lax.rem(dp + k, 8), pr)

    def proto_peer(dy, dz):
        return (dp, lax.rem(y + dy, NY) * NZ + lax.rem(z + dz, NZ))

    def remote(src, dst, ssem, rsem, device):
        return pltpu.make_async_remote_copy(
            src, dst, ssem, rsem, device_id=device, device_id_type=MESH
        )

    def wait_bytes(ref, sem):
        pltpu.make_async_copy(ref, ref, sem).wait()

    def load(src, dst, sem, parts):
        size = src.shape[0] // parts
        for i in range(parts):
            rows = pl.ds(i * size, size)
            pltpu.make_async_copy(src.at[rows], dst.at[rows], sem).start()

    load(index_hbm, index_v, in_sem.at[0], 1)
    load(teacher_hbm, teacher_v, in_sem.at[1], 4)
    barrier = pltpu.get_barrier_semaphore()
    for k in range(1, 8):
        pl.semaphore_signal(barrier, inc=1, device_id=dp_peer(k), device_id_type=MESH)
    for dy, dz in FAR_FIRST:
        pl.semaphore_signal(
            barrier, inc=1, device_id=proto_peer(dy, dz), device_id_type=MESH
        )
    for j in range(4):
        cols = pl.ds(2 * W * j, 2 * W)
        pltpu.make_async_copy(protos_hbm.at[:, cols], protos_v.at[j], protos_sem.at[j]).start()
    load(student_hbm, student_v, in_sem.at[3], 4)

    wait_bytes(index_v, in_sem.at[0])
    for i in range(4):
        places = lax.broadcasted_iota(jnp.int32, (256, 128), 0)
        onehot[i] = jnp.where(places == index_v[i : i + 1, :], 1.0, 0.0).astype(BF16)

    def masked(patches, i):
        rows = lax.dot_general(
            onehot[i], patches[256 * i : 256 * i + 256, :],
            (((0,), (0,)), ((), ())), preferred_element_type=F32,
        )
        norm = jnp.sqrt(jnp.sum(rows * rows, axis=1, keepdims=True) + epsilon)
        return rows / norm, norm

    wait_bytes(teacher_v, in_sem.at[1])
    for i in range(4):
        unit, _ = masked(teacher_v, i)
        t_send[128 * i : 128 * i + 128, :] = unit
        t_cast[128 * i : 128 * i + 128, :] = unit.astype(BF16)

    def put_cols(buf, slot, j, sums):
        for q in range(W // 128):
            buf[slot, pl.ds(4 * j + q, 1), :] = sums[:, 128 * q : 128 * q + 128]


    def send_cols(t, q):
        piece = cbuf.at[t, dp, pl.ds(pl.multiple_of(8 * q, 8), 8)]
        for k in (4, 3, 5, 2, 6, 1, 7):
            remote(piece, piece, c_ssem, c_rsem.at[t, q], dp_peer(k)).start()

    def take_cols(t, q):
        rows = slice(8 * q, 8 * q + 8)
        wait_bytes(cbuf.at[t, pl.ds(0, 7), rows], c_rsem.at[t, q])
        vrow[rows, :] = 1.0 / jnp.sum(cbuf[t, :, rows, :], axis=0)

    def front(p, carry):
        for i in range(2):
            wait_bytes(protos_v.at[2 * p + i], protos_sem.at[2 * p + i])
        for i in range(4):
            j = 4 * p + i
            cols = pl.ds(pl.multiple_of(j * W, W), W)
            weights = protos_v[2 * p + i // 2, :, W * (i % 2) : W * (i % 2) + W].astype(F32)
            inv = 1.0 / jnp.sqrt(jnp.sum(weights * weights, axis=0, keepdims=True) + epsilon)
            pinv[:, cols] = inv
            unit = (weights * inv).astype(BF16)
            pc[:, cols] = unit
            block = jnp.exp2(dot(t_cast[...], unit) * teacher_scale)
            expos[:, cols] = block
            put_cols(cbuf.at[0], dp, j, jnp.sum(block, axis=0, keepdims=True))
        return carry

    def low_part(q, carry):
        for i in range(2):
            cols = pl.ds(pl.multiple_of((2 * q + i) * W, W), W)
            unit = protos_v[q, :, W * i : W * i + W].astype(F32) * pinv[:, cols]
            plo[:, cols] = (unit - pc[:, cols].astype(F32)).astype(BF16)
        return carry

    lax.fori_loop(0, 2, front, 0)
    pl.semaphore_wait(barrier, 7 + len(FAR_FIRST))
    for q in range(4):
        send_cols(0, q)

    def send_rows(t):
        for dy, dz in FAR_FIRST:
            remote(rbuf.at[t, pr], rbuf.at[t, pr], r_ssem, r_rsem.at[t], proto_peer(dy, dz)).start()

    def take_rows(t):
        wait_bytes(rbuf.at[t, pl.ds(0, 31)], r_rsem.at[t])
        return jnp.sum(rbuf[t], axis=0)

    def spread(row):
        return jnp.transpose(jnp.broadcast_to(row, (128, 128)))

    def row_pass(t):
        for p in range(4):
            take_cols(t, p)
            for i in range(4):
                rows = slice(128 * i, 128 * i + 128)
                total = row_acc[rows, :] if p else jnp.zeros((128, 128), F32)
                for k in range(8 * p, 8 * p + 8):
                    total += expos[rows, 128 * k : 128 * k + 128] * vrow[k : k + 1, :]
                if p < 3:
                    row_acc[rows, :] = total
                else:
                    rbuf[t, pr, i : i + 1, :] = jnp.sum(
                        jnp.transpose(total), axis=0, keepdims=True
                    )

    def col_pass(t):
        def chunk(j, carry):
            cols = pl.ds(pl.multiple_of(j * 1024, 1024), 1024)
            sums = jnp.zeros((8, 1024), F32)
            for i in range(64):
                scale = ub[8 * i : 8 * i + 8, :]
                sums += expos[8 * i : 8 * i + 8, cols] * jnp.concatenate([scale] * 8, axis=1)
            total = jnp.sum(sums, axis=0, keepdims=True)
            for q in range(8):
                cbuf[t, dp, pl.ds(8 * j + q, 1), :] = total[:, 128 * q : 128 * q + 128]
            send_cols(t, j)
            return carry

        lax.fori_loop(0, 4, chunk, 0)

    def spread_rows(values, target):
        for i in range(4):
            target[128 * i : 128 * i + 128, :] = spread(values[i : i + 1, :])

    wait_bytes(student_v, in_sem.at[3])
    for i in range(4):
        unit, norm = masked(student_v, i)
        rows = slice(128 * i, 128 * i + 128)
        s_send[rows, :] = unit
        s_cast[rows, :] = unit.astype(BF16)
        s_inv[rows, :] = jnp.broadcast_to(1.0 / norm, (128, 128))
        s_unit_t[:, rows] = jnp.transpose(unit)
    ts = [
        remote(t_send, t_other, ts_ssem.at[0], ts_rsem.at[0], partner),
        remote(s_send, s_other, ts_ssem.at[1], ts_rsem.at[1], partner),
    ]
    for copy in ts:
        copy.start()

    half = core * 2048
    tot_acc[...] = jnp.zeros_like(tot_acc)
    fp[...] = jnp.zeros_like(fp)

    def student_cols(j, keep):
        at = lax.rem(j * W + half, 4096)
        cols = pl.ds(pl.multiple_of(at, W), W)
        block = jnp.exp2(dot(s_cast[...], pc[:, cols]) * student_scale)
        for q in range(W // 128):
            tot_acc[...] += block[:, 128 * q : 128 * q + 128]
        high, low = split(block)
        if keep:
            mine = pl.ds(pl.multiple_of(j * W, W), W)
            x2h[0:512, mine] = high
            x2l[0:512, mine] = low
        fp[...] += (
            dot_cols(high, pc[:, cols]) + dot_cols(low, pc[:, cols]) + dot_cols(high, plo[:, cols])
        )

    def student_mine(j, carry):
        student_cols(j, True)
        return carry

    def student_rest(j, carry):
        student_cols(j, False)
        return carry

    lax.fori_loop(0, 4, low_part, 0)
    lax.fori_loop(0, 2, student_mine, 0)
    row_pass(0)
    send_rows(0)

    lax.fori_loop(2, 4, student_mine, 0)
    lax.fori_loop(4, 8, student_rest, 0)
    for i in range(4):
        rbuf[3, pr, i : i + 1, :] = jnp.sum(
            jnp.transpose(tot_acc[128 * i : 128 * i + 128, :]), axis=0, keepdims=True
        )
    send_rows(3)
    spread_rows(1.0 / take_rows(0), ub)
    col_pass(1)

    def send_y(q, src, steps):
        for dy in steps:
            ty = lax.rem(y + dy, NY)
            remote(
                src.at[pl.ds(pl.multiple_of(ty * 128, 128), 128)], yr.at[q, dy - 1],
                y_ssem.at[q], y_rsem.at[q], proto_peer(dy, 0),
            ).start()

    def take_y(q, src):
        wait_bytes(yr.at[q], y_rsem.at[q])
        own = pl.ds(pl.multiple_of(y * 128, 128), 128)
        ysum[q] = src[own, :] + yr[q, 0] + yr[q, 1] + yr[q, 2]

    def send_z(q):
        for dz in (4, 3, 5, 2, 6, 1, 7):
            tz = lax.rem(z + dz, NZ)
            remote(
                ysum.at[q, pl.ds(pl.multiple_of(tz * 16, 16), 16)], zr.at[q, dz - 1],
                z_ssem, z_rsem.at[q], proto_peer(0, dz),
            ).start()

    def take_z(q):
        wait_bytes(zr.at[q], z_rsem.at[q])
        total = ysum[q, pl.ds(pl.multiple_of(z * 16, 16), 16), :]
        for k in range(7):
            total += zr[q, k]
        return total

    send_y(0, fp, (2,))
    for copy in ts:
        copy.wait_recv()
    t_cast[...] = t_other[...].astype(BF16)
    s_cast[...] = s_other[...].astype(BF16)

    def other_cols(j, carry):
        cols = pl.ds(pl.multiple_of(j * W + half, W), W)
        mine = pl.ds(pl.multiple_of(j * W, W), W)
        high, low = split(jnp.exp2(dot(t_cast[...], pc[:, cols]) * teacher_scale))
        e2h[512:1024, mine] = high
        e2l[512:1024, mine] = low
        high, low = split(jnp.exp2(dot(s_cast[...], pc[:, cols]) * student_scale))
        x2h[512:1024, mine] = high
        x2l[512:1024, mine] = low
        return carry

    lax.fori_loop(0, 4, other_cols, 0)
    for i in range(4):
        s_unit_t[:, 512 + 128 * i : 640 + 128 * i] = jnp.transpose(
            s_other[128 * i : 128 * i + 128, :]
        )
    row_pass(1)
    send_rows(1)

    def scale_half(at, ref):
        for i in range(4):
            cols = slice(at + 128 * i, at + 128 * i + 128)
            high, low = split(s_unit_t[:, cols] * ref[i : i + 1, :])
            a_hi[:, cols] = high
            a_lo[:, cols] = low

    tot_row[...] = 1.0 / take_rows(3)
    swap_s[0] = tot_row[...]
    swap_tot = remote(swap_s.at[0], swap_r.at[0], swap_ssem.at[0], swap_rsem.at[0], partner)
    swap_tot.start()
    spread_rows(tot_row[...], totb)
    def weigh_some(rows, cols, high, low):
        return (
            dot(a_hi[:, rows], high[rows, cols])
            + dot(a_lo[:, rows], high[rows, cols])
            + dot(a_hi[:, rows], low[rows, cols])
        )

    scale_half(0, tot_row)

    def probs_own(j, carry):
        mine = pl.ds(pl.multiple_of(j * W, W), W)
        wtp[:, mine] = weigh_some(slice(0, 512), mine, x2h, x2l)
        return carry

    lax.fori_loop(0, 4, probs_own, 0)
    swap_tot.wait_recv()
    scale_half(512, swap_r.at[0])

    def probs_other(j, carry):
        mine = pl.ds(pl.multiple_of(j * W, W), W)
        wtp[:, mine] += weigh_some(slice(512, 1024), mine, x2h, x2l)
        return carry

    lax.fori_loop(0, 4, probs_other, 0)
    spread_rows(1.0 / take_rows(1), ub)
    col_pass(2)

    send_y(0, fp, (1, 3))
    def own_split(j, carry):
        cols = pl.ds(pl.multiple_of(j * W + half, W), W)
        mine = pl.ds(pl.multiple_of(j * W, W), W)
        high, low = split(expos[:, cols])
        e2h[0:512, mine] = high
        e2l[0:512, mine] = low
        return carry

    lax.fori_loop(0, 4, own_split, 0)
    row_pass(2)
    send_rows(2)

    ft[...] = jnp.zeros_like(ft)

    def target_cols(q, carry):
        total = ft[...]
        for i in range(2):
            j = 2 * q + i
            cols = pl.ds(pl.multiple_of(j * W, W), W)
            inv = pinv[:, cols]
            scale = jnp.concatenate(
                [
                    inv[:, 128 * n : 128 * n + 128] * vrow[pl.ds(4 * j + n, 1), :]
                    for n in range(W // 128)
                ],
                axis=1,
            )
            b_high, b_low = split(protos_v[q, :, W * i : W * i + W].astype(F32) * scale)
            high, low = split(expos[:, cols])
            total += dot_cols(high, b_high) + dot_cols(low, b_high) + dot_cols(high, b_low)
        ft[...] = total
        return carry

    lax.fori_loop(0, 2, target_cols, 0)
    take_y(0, fp)
    send_z(0)
    lax.fori_loop(2, 4, target_cols, 0)
    for n, dz in enumerate(Z_FAR_FIRST):
        tz = lax.rem(z + dz, NZ) * 16
        for dy in (2, 1, 3):
            ty = lax.rem(y + dy, NY) * 128
            remote(
                ft.at[pl.ds(pl.multiple_of(ty + tz, 16), 16)], yr.at[1, dy - 1, pl.ds(pl.multiple_of(tz, 16), 16)],
                yp_ssem, yp_rsem.at[n // 4], proto_peer(dy, 0),
            ).start()
    swap_s[1] = 1.0 / take_rows(2)
    swap_u = remote(swap_s.at[1], swap_r.at[1], swap_ssem.at[1], swap_rsem.at[1], partner)
    swap_u.start()
    def block(d, offset, size):
        return pl.ds(pl.multiple_of(d * 64 + offset, 32), size)

    def protos_part(j, target):
        mine = pl.ds(pl.multiple_of(j * V, V), V)
        cols = pl.ds(pl.multiple_of(j * V + half, V), V)
        at = half // 128 + V // 128 * j
        target = jnp.concatenate(
            [
                target[:, 128 * q : 128 * q + 128] * vrow[pl.ds(at + q, 1), :]
                for q in range(V // 128)
            ],
            axis=1,
        )
        total = wtp[:, mine] - target
        inside = pl.ds(pl.multiple_of(lax.rem(j, 4) * V, V), V)
        unit = protos_v[2 * core + lax.div(j, 4), :, inside].astype(F32) * pinv[:, cols]
        inner = jnp.sum(unit * total, axis=0, keepdims=True)
        gpart[j] = (total - unit * inner) * (pinv[:, cols] * slope_scale)
        remote(gpart.at[j, block(x_far, 0, 32)], p1r.at[j, 0], p1_ssem, p1_rsem.at[j], right).start()
        remote(gpart.at[j, block(x_far, 32, 32)], p1r.at[j, 1], p1_ssem, p1_rsem.at[j], left).start()
        remote(gpart.at[j, block(x, 32 - 32 * core, 32)], p2r.at[j, 4], p2_ssem, p2_rsem.at[j], partner).start()

    first = pl.ds(0, V)
    scale_half(0, swap_s.at[1])
    target = weigh_some(slice(0, 512), first, e2h, e2l)
    swap_u.wait_recv()
    scale_half(512, swap_r.at[1])
    protos_part(0, target + weigh_some(slice(512, 1024), first, e2h, e2l))

    def protos_rest(j, carry):
        protos_part(j, weigh_some(slice(0, 1024), pl.ds(pl.multiple_of(j * V, V), V), e2h, e2l))
        return carry

    def take_pieces(first, last):
        wait_bytes(yr.at[1, pl.ds(0, 3), pl.ds(0, 64)], yp_rsem.at[first // 4])
        for dz in Z_FAR_FIRST[first:last]:
            tz = lax.rem(z + dz, NZ) * 16
            rows = pl.ds(pl.multiple_of(tz, 16), 16)
            own = pl.ds(pl.multiple_of(y * 128 + tz, 16), 16)
            ysum[1, rows, :] = ft[own, :] + yr[1, 0, rows, :] + yr[1, 1, rows, :] + yr[1, 2, rows, :]
            if dz:
                remote(
                    ysum.at[1, rows], zr.at[1, dz - 1], z_ssem, z_rsem.at[1], proto_peer(0, dz)
                ).start()

    def pass_on(j, carry):
        wait_bytes(p1r.at[j], p1_rsem.at[j])
        for s, side in enumerate((x_next, x_prev)):
            gpart[j, block(side, 32 * s, 32), :] += p1r[j, s]
            for c in range(2):
                remote(
                    gpart.at[j, block(side, 32 * c, 32)], p2r.at[j, 2 * s + core],
                    p2_ssem, p2_rsem.at[j], (side * 2 + c, pr),
                ).start()
        return carry

    lax.fori_loop(1, 5, protos_rest, 0)
    pass_on(0, 0)
    take_pieces(0, 4)
    lax.fori_loop(5, 8, protos_rest, 0)

    lax.fori_loop(1, 4, pass_on, 0)
    take_pieces(4, 8)
    lax.fori_loop(4, 6, pass_on, 0)
    spread_rows(swap_s[1], ub)

    own16 = pl.ds(pl.multiple_of(y * 128 + z * 16, 16), 16)
    by_probs = take_z(0)
    by_target = take_z(1)
    unit = s_send[own16, :]
    scale_p = jnp.concatenate([totb[own16, :]] * 2, axis=1)
    scale_t = jnp.concatenate([ub[own16, :]] * 2, axis=1)
    grad = slope_scale * (by_probs * scale_p - by_target * scale_t)
    inner = jnp.sum(unit * grad, axis=1, keepdims=True)
    ag[y, z] = (grad - unit * inner) * jnp.concatenate([s_inv[own16, :]] * 2, axis=1)
    for dz in (1, 7, 2, 6, 3, 5, 4):
        remote(ag.at[y, z], ag.at[y, z], agz_ssem, agz_rsem.at[dz - 1], proto_peer(0, dz)).start()

    def to_y(piece):
        for dy in (2, 1, 3):
            remote(piece, piece, agy_ssem, agy_rsem.at[dy - 1], proto_peer(dy, 0)).start()

    to_y(ag.at[y, z])
    lax.fori_loop(6, 8, pass_on, 0)

    def finish(j, carry):
        wait_bytes(p2r.at[j], p2_rsem.at[j])
        gw_hbm[:, pl.ds(pl.multiple_of(j * V + half, V), V)] = (
            gpart[j, block(x, 32 * core, 32), :] + p2r[j, core] + p2r[j, 2 + core]
        )
        gw_hbm[:, pl.ds(pl.multiple_of(j * V + 2048 - half, V), V)] = (
            p2r[j, 4] + p2r[j, 1 - core] + p2r[j, 3 - core]
        )
        return carry

    for dz in (1, 7, 2, 6, 3, 5, 4):
        piece = ag.at[y, lax.rem(z + NZ - dz, NZ)]
        wait_bytes(piece, agz_rsem.at[dz - 1])
        to_y(piece)
    rows_hbm[y] = ag[y]
    lax.fori_loop(0, 8, finish, 0)

    for dy in (1, 3, 2):
        image = lax.rem(y + NY - dy, NY)
        wait_bytes(ag.at[image], agy_rsem.at[dy - 1])
        rows_hbm[image] = ag[image]

    wait_bytes(cbuf.at[:, pl.ds(0, 7)], c_ssem)
    wait_bytes(rbuf.at[:, pl.ds(0, 31)], r_ssem)
    for copy in ts:
        copy.wait_send()
    swap_tot.wait_send()
    swap_u.wait_send()
    wait_bytes(yr.at[0], y_ssem.at[0])
    wait_bytes(yr.at[1], yp_ssem)
    wait_bytes(zr, z_ssem)
    wait_bytes(ag.at[0, pl.ds(0, 7)], agz_ssem)
    wait_bytes(ag.at[pl.ds(0, 3)], agy_ssem)

    wait_bytes(p1r, p1_ssem)
    wait_bytes(p2r, p2_ssem)


def place_kernel(rows, index, gw, gp_hbm, gw_hbm, placed, out_sem):
    stores = [pltpu.make_async_copy(gw, gw_hbm, out_sem.at[4])]
    stores[0].start()
    for i in range(4):
        places = lax.broadcasted_iota(jnp.int32, (256, 128), 0)
        onehot = jnp.where(places == index[i : i + 1, :], 1.0, 0.0).astype(BF16)
        high, low = split(rows[i].reshape(128, 256))
        placed[i] = dot(onehot, high) + dot(onehot, low)
        stores.append(
            pltpu.make_async_copy(placed.at[i], gp_hbm.at[pl.ds(256 * i, 256)], out_sem.at[i])
        )
        stores[-1].start()
    for copy in stores:
        copy.wait()


def body(student_patches, teacher_patches, masked_index, prototypes):
    dma = pltpu.SemaphoreType.DMA

    def vmem(*shape, dtype=F32):
        return pltpu.VMEM(shape, dtype)

    def half_vmem(*shape):
        return pltpu.VMEM(shape, BF16)

    scratch = [
        half_vmem(1024, 256), half_vmem(1024, 256), vmem(4, 128, dtype=jnp.int32), half_vmem(4, 256, 1024), dma((4,)), dma((4,)),
        half_vmem(4, 256, 128), vmem(512, 256), vmem(512, 256), vmem(512, 256), vmem(512, 256),
        half_vmem(512, 256), half_vmem(512, 256), vmem(256, 1024), vmem(512, 128),
        half_vmem(256, 4096), half_vmem(256, 4096), vmem(1, 4096), vmem(512, 4096),
        half_vmem(1024, 2048), half_vmem(1024, 2048), half_vmem(1024, 2048), half_vmem(1024, 2048),
        vmem(256, 2048), half_vmem(256, 1024), half_vmem(256, 1024),
        vmem(3, 8, 32, 128), dma, dma((3, 4)),
        vmem(4, 32, 4, 128), dma, dma((4,)),
        vmem(512, 128), vmem(512, 128), vmem(32, 128), vmem(4, 128), vmem(512, 128), vmem(512, 128),
        dma((2,)), dma((2,)), vmem(2, 4, 128), vmem(2, 4, 128), dma((2,)), dma((2,)),
        vmem(512, 256), vmem(512, 256), vmem(2, 3, 128, 256), vmem(2, 128, 256), dma((1,)), dma((1,)), dma, dma((2,)),
        vmem(2, 7, 16, 256), dma, dma((2,)),
        vmem(4, 8, 16, 256), dma, dma((7,)), dma, dma((3,)),
        vmem(8, 256, 256), vmem(8, 2, 32, 256), dma, dma((8,)),
        vmem(8, 5, 32, 256), dma, dma((8,)),
    ]
    anywhere = pl.BlockSpec(memory_space=pl.ANY)
    rows, grad_prototypes = pl.pallas_call(
        kernel,
        out_shape=(
            pltpu.VMEM((4, 8, 16, 256), F32),
            pltpu.VMEM((32, 4096), F32),
        ),
        in_specs=[anywhere] * 4,
        out_specs=(pl.BlockSpec(memory_space=pltpu.VMEM),) * 2,
        scratch_shapes=scratch,
        compiler_params=pltpu.CompilerParams(
            collective_id=0, has_side_effects=True, vmem_limit_bytes=60 * 1024 * 1024
        ),
    )(student_patches, teacher_patches, masked_index, prototypes)
    return pl.pallas_call(
        place_kernel,
        out_shape=(
            jax.ShapeDtypeStruct((1024, 256), F32),
            jax.ShapeDtypeStruct((32, 4096), F32),
        ),
        in_specs=[pl.BlockSpec(memory_space=pltpu.VMEM)] * 3,
        out_specs=(anywhere, anywhere),
        scratch_shapes=[vmem(4, 256, 256), dma((5,))],
    )(
        pltpu.with_memory_space_constraint(rows, pltpu.VMEM),
        masked_index,
        pltpu.with_memory_space_constraint(grad_prototypes, pltpu.VMEM),
    )


def solution(mesh):
    placed = (P("dp", None), P("dp", None), P("dp", None), P(None, "proto"))
    return jax.shard_map(
        body,
        mesh=mesh,
        in_specs=placed,
        out_specs=(P("dp", None), P("dp", "proto")),
        check_vma=False,
    )
```
